32 devices in a mesh: dp: 8 (over z, y), tensor: 4 (over x, core).
Axes of the slice: x: 2, y: 2, z: 4, core: 2. Of those that a mesh axis runs over, the one named last changes fastest.
Arguments:
- tokens: bfloat16 [32, 197, 768], P('dp'), may hold values from -6 to 6
- ln1_gain: float32 [768], replicated, may hold values from 0.5 to 1.5
- ln1_shift: float32 [768], replicated, may hold values from -1.75 to 1.75
- w_query: bfloat16 [768, 768], P(None, 'tensor'), may hold values from -0.21875 to 0.21875
- b_query: float32 [768], P('tensor'), may hold values from -1.25 to 1.25
- w_key: bfloat16 [768, 768], P(None, 'tensor'), may hold values from -0.21875 to 0.21875
- w_value: bfloat16 [768, 768], P(None, 'tensor'), may hold values from -0.21875 to 0.21875
- b_value: float32 [768], P('tensor'), may hold values from -1.25 to 1.25
- w_proj: bfloat16 [768, 768], P('tensor'), may hold values from -0.875 to 0.875
- b_proj: float32 [768], replicated, may hold values from -1.75 to 1.75
- ln2_gain: float32 [768], replicated, may hold values from 0.5 to 1.5
- ln2_shift: float32 [768], replicated, may hold values from -1.75 to 1.75
- w_fc1: bfloat16 [768, 3072], P(None, 'tensor'), may hold values from -0.21875 to 0.21875
- b_fc1: float32 [3072], P('tensor'), may hold values from -1.75 to 1.75
- w_fc2: bfloat16 [3072, 768], P('tensor'), may hold values from -0.109375 to 0.109375
- b_fc2: float32 [768], replicated, may hold values from -1.75 to 1.75
- cotangent: bfloat16 [32, 197, 768], P('dp'), may hold values from -6 to 6
Outputs:
- layer_out: bfloat16 [32, 197, 768], P('dp')
- tokens_grad: bfloat16 [32, 197, 768], P('dp')
- ln1_gain_grad: float32 [768], replicated
- ln1_shift_grad: float32 [768], replicated
- w_query_grad: float32 [768, 768], P(None, 'tensor')
- b_query_grad: float32 [768], P('tensor')
- w_key_grad: float32 [768, 768], P(None, 'tensor')
- w_value_grad: float32 [768, 768], P(None, 'tensor')
- b_value_grad: float32 [768], P('tensor')
- w_proj_grad: float32 [768, 768], P('tensor')
- b_proj_grad: float32 [768], replicated
- ln2_gain_grad: float32 [768], replicated
- ln2_shift_grad: float32 [768], replicated
- w_fc1_grad: float32 [768, 3072], P(None, 'tensor')
- b_fc1_grad: float32 [3072], P('tensor')
- w_fc2_grad: float32 [3072, 768], P('tensor')
- b_fc2_grad: float32 [768], replicated
The draws below stay inside these ranges and needn't reach their ends.
All inputs are finite; a program needn't handle non-finite values.
Results may differ from the reference program's by a relative error of at most 0.012.
The reference program's roundings to bfloat16 on the way count: a program that leaves them out, or rounds other values in their place, can miss the bound.
Values may be sent and summed in bfloat16 or wider, within the bound.
A program may use at most 128 MiB of HBM per device.

```python
import jax
import jax.numpy as jnp
from jax import lax

HEADS = 12
HEAD_DIM = 64
D = 768
FF = 3072
SEQ = 197
IMAGES = 32


def levels(own_key, dims, cuts, smallest, largest):
    factor_of = 1.0
    for position, shards_of in cuts:
        steps = jax.random.uniform(jax.random.fold_in(jax.random.fold_in(own_key, 6), position), (shards_of,), jnp.float32, smallest / len(cuts), largest / len(cuts))
        factor_of = factor_of * jnp.repeat(jnp.exp(steps), dims[position] // shards_of).reshape((-1,) + (1,) * (len(dims) - 1 - position))
    return factor_of


def bell_draw(own_key, dims, scale, bound, shards=(), dtype=jnp.bfloat16):
    array = jax.random.normal(own_key, dims, jnp.float32) * scale
    if len(shards) > 0:
        array = levels(own_key, dims, shards, -0.22, 0.18) * array
    return jnp.clip(array, min=-bound, max=bound).astype(dtype)


def setup_inputs(seed: int = 0) -> dict:
    arg_keys = jax.random.split(jax.random.key(seed), 18)
    tokens = bell_draw(arg_keys[0], (IMAGES, SEQ, D), 1.0, 6.0, ((0, 8),))
    ln1_gain = jnp.clip(1.0 + 0.1 * jax.random.normal(arg_keys[1], (D,), jnp.float32), 0.5, 1.5)
    ln1_shift = bell_draw(arg_keys[2], (D,), 0.3, 1.75, (), jnp.float32)
    w_query = bell_draw(arg_keys[3], (D, D), D ** -0.5, 0.21875, ((1, 4),))
    b_query = bell_draw(arg_keys[4], (D,), 0.2, 1.25, ((0, 4),), jnp.float32)
    w_key = bell_draw(arg_keys[5], (D, D), D ** -0.5, 0.21875, ((1, 4),))
    w_value = bell_draw(arg_keys[6], (D, D), D ** -0.5, 0.21875, ((1, 4),))
    b_value = bell_draw(arg_keys[7], (D,), 0.2, 1.25, ((0, 4),), jnp.float32)
    w_proj = bell_draw(arg_keys[8], (D, D), (D // 16) ** -0.5, 0.875, ((0, 4),))
    b_proj = bell_draw(arg_keys[9], (D,), 0.3, 1.75, (), jnp.float32)
    ln2_gain = jnp.clip(1.0 + 0.1 * jax.random.normal(arg_keys[10], (D,), jnp.float32), 0.5, 1.5)
    ln2_shift = bell_draw(arg_keys[11], (D,), 0.3, 1.75, (), jnp.float32)
    w_fc1 = bell_draw(arg_keys[12], (D, FF), D ** -0.5, 0.21875, ((1, 4),))
    b_fc1 = bell_draw(arg_keys[13], (FF,), 0.3, 1.75, ((0, 4),), jnp.float32)
    w_fc2 = bell_draw(arg_keys[14], (FF, D), FF ** -0.5, 0.109375, ((0, 4),))
    b_fc2 = bell_draw(arg_keys[15], (D,), 0.3, 1.75, (), jnp.float32)
    cotangent = bell_draw(arg_keys[16], (IMAGES, SEQ, D), 1.0, 6.0, ((0, 8),))
    return {"tokens": tokens, "ln1_gain": ln1_gain, "ln1_shift": ln1_shift, "w_query": w_query, "b_query": b_query, "w_key": w_key, "w_value": w_value, "b_value": b_value, "w_proj": w_proj, "b_proj": b_proj, "ln2_gain": ln2_gain, "ln2_shift": ln2_shift, "w_fc1": w_fc1, "b_fc1": b_fc1, "w_fc2": w_fc2, "b_fc2": b_fc2, "cotangent": cotangent}


@jax.custom_vjp
def low(v):
    return lax.optimization_barrier(v.astype(jnp.bfloat16)).astype(jnp.float32)

@jax.custom_vjp
def low_back(v):
    return v

def low_keep(v):
    return (low(v), None)

def low_pass(kept, grad):
    return (grad,)

def back_keep(v):
    return (v, None)

def back_low(kept, grad):
    return (low(grad),)
low.defvjp(low_keep, low_pass)
low_back.defvjp(back_keep, back_low)
EPSILON = 1e-06
HIGHEST = lax.Precision.HIGHEST

def layer_norm(values, gain, shift):
    center = values - lax.optimization_barrier(jnp.mean(values, axis=-1, keepdims=True))
    spread = lax.optimization_barrier(jnp.mean(center * center, axis=-1, keepdims=True))
    return center * lax.rsqrt(spread + EPSILON) * gain + shift

def forward(tokens, ln1_gain, ln1_shift, w_query, b_query, w_key, w_value, b_value, w_proj, b_proj, ln2_gain, ln2_shift, w_fc1, b_fc1, w_fc2, b_fc2):
    images, length, model_width = tokens.shape
    flat_rows = tokens.reshape(images * length, model_width)
    normed = low(layer_norm(flat_rows, ln1_gain, ln1_shift))
    query = low_back(low(jnp.dot(normed, w_query, precision=HIGHEST) + b_query))
    keys = low_back(low(jnp.dot(normed, w_key, precision=HIGHEST)))
    values = low_back(low(jnp.dot(normed, w_value, precision=HIGHEST) + b_value))
    shape4 = (images, length, HEADS, HEAD_DIM)
    scores = low_back(jnp.einsum('bqhd,bkhd->bhqk', query.reshape(shape4), keys.reshape(shape4), precision=HIGHEST) * HEAD_DIM ** (-0.5))
    probs = jax.nn.softmax(scores, axis=-1)
    mixed = jnp.einsum('bhqk,bkhd->bqhd', low(probs), values.reshape(shape4), precision=HIGHEST)
    mixed = low_back(low(mixed.reshape(images * length, model_width)))
    attn = low_back(jnp.dot(mixed, w_proj, precision=HIGHEST))
    resid = flat_rows + attn + b_proj
    middle = low(layer_norm(resid, ln2_gain, ln2_shift))
    hidden = low_back(jnp.dot(middle, w_fc1, precision=HIGHEST) + b_fc1)
    active = low(jax.nn.gelu(hidden, approximate=False))
    branch = low_back(jnp.dot(active, w_fc2, precision=HIGHEST))
    return (resid + branch + b_fc2).reshape(tokens.shape)

def reference(tokens, ln1_gain, ln1_shift, w_query, b_query, w_key, w_value, b_value, w_proj, b_proj, ln2_gain, ln2_shift, w_fc1, b_fc1, w_fc2, b_fc2, cotangent):
    inputs = [tokens, ln1_gain, ln1_shift, w_query, b_query, w_key, w_value, b_value, w_proj, b_proj, ln2_gain, ln2_shift, w_fc1, b_fc1, w_fc2, b_fc2]
    inputs = [item.astype(jnp.float32) for item in inputs]
    result, pullback = jax.vjp(forward, *inputs)
    grads = pullback(cotangent.astype(jnp.float32))
    return (result.astype(jnp.bfloat16), grads[0].astype(jnp.bfloat16), grads[1], grads[2], grads[3], grads[4], grads[5], grads[6], grads[7], grads[8], grads[9], grads[10], grads[11], grads[12], grads[13], grads[14], grads[15])
```

```python
import jax
import jax.numpy as jnp
from jax import lax
from jax.experimental import pallas as pl
from jax.experimental.pallas import tpu as pltpu
from jax.sharding import PartitionSpec as P

HEAD_DIM = 64
EPSILON = 1e-06
BF16 = jnp.bfloat16
F32 = jnp.float32
MESH = pl.DeviceIdType.MESH
VMEM_LIMIT = 56 * 1024 * 1024


def matmul(left, right):
    return jnp.dot(left, right, preferred_element_type=F32)


def inner_rows(left, right):
    return lax.dot_general(left, right, (((0,), (0,)), ((), ())), preferred_element_type=F32)


def times_transpose(left, right):
    return lax.dot_general(left, right, (((1,), (1,)), ((), ())), preferred_element_type=F32)


def normalize(values):
    center = values - jnp.mean(values, axis=-1, keepdims=True)
    scale = lax.rsqrt(jnp.mean(center * center, axis=-1, keepdims=True) + EPSILON)
    return center * scale, scale


def norm_back(hat, scale, gain, grad):
    inner = grad * gain
    return scale * (
        inner
        - jnp.mean(inner, axis=-1, keepdims=True)
        - hat * jnp.mean(inner * hat, axis=-1, keepdims=True)
    )


def soft_probs(query, keys, length):
    scores = times_transpose(query, keys) * (HEAD_DIM**-0.5)
    column = lax.broadcasted_iota(jnp.int32, scores.shape, 1)
    scores = jnp.where(column < length, scores, -1e30)
    raised = jnp.exp(scores - jnp.max(scores, axis=-1, keepdims=True))
    return raised * (1.0 / jnp.sum(raised, axis=-1, keepdims=True))


def attention_kernel(
    length, x_ref, gain, shift, wq, bq, wk, wv, bv, wp, a_ref, q_ref, k_ref, v_ref, o_ref, part_ref
):
    hat, _ = normalize(x_ref[0].astype(F32))
    normed = (hat * gain[...] + shift[...]).astype(BF16)
    a_ref[0] = normed
    query = (matmul(normed, wq[...]) + bq[...]).astype(BF16)
    keys = matmul(normed, wk[...]).astype(BF16)
    values = (matmul(normed, wv[...]) + bv[...]).astype(BF16)
    q_ref[0] = query
    k_ref[0] = keys
    v_ref[0] = values
    heads = []
    for head in range(query.shape[1] // HEAD_DIM):
        span = slice(head * HEAD_DIM, (head + 1) * HEAD_DIM)
        probs = soft_probs(query[:, span], keys[:, span], length)
        heads.append(matmul(probs.astype(BF16), values[:, span]))
    mixed = jnp.concatenate(heads, axis=1).astype(BF16)
    o_ref[0] = mixed
    part_ref[0] = matmul(mixed, wp[...]).astype(BF16)


def feed_kernel(c_ref, g_ref, w1, b1, w2, part_ref, fc_ref, bias_ref, acc1, acc2):
    step = pl.program_id(0)
    rows = c_ref.shape[1]
    width = c_ref.shape[2]

    @pl.when(step == 0)
    def _():
        acc1[...] = jnp.zeros_like(acc1)
        acc2[...] = jnp.zeros_like(acc2)
        bias_ref[...] = jnp.zeros_like(bias_ref)

    middle = c_ref[0]
    grad = g_ref[0]
    hidden = matmul(middle, w1[...]) + b1[...]
    cdf = 0.5 * (1.0 + lax.erf(hidden * (0.5**0.5)))
    slope = cdf + hidden * jnp.exp(-0.5 * hidden * hidden) * 0.3989422804014327
    active = (hidden * cdf).astype(BF16)
    grad_hidden = (times_transpose(grad, w2[...]) * slope).astype(BF16)
    part_ref[0, :rows] = matmul(active, w2[...]).astype(BF16)
    part_ref[0, rows:] = times_transpose(grad_hidden, w1[...]).astype(BF16)
    acc2[...] += inner_rows(active, grad)
    acc1[...] += inner_rows(middle, grad_hidden)
    bias_ref[...] += jnp.sum(grad_hidden.astype(F32), axis=0, keepdims=True)

    @pl.when(step == pl.num_programs(0) - 1)
    def _():
        fc_ref[:width] = acc1[...].astype(BF16)
        fc_ref[width:] = acc2[...].astype(BF16)


def back_kernel(
    length, h_ref, o_ref, a_ref, q_ref, k_ref, v_ref, wp, wq, wk, wv,
    part_ref, gq_ref, gk_ref, gv_ref, gp_ref, bq_ref, bv_ref, accq, acck, accv, accp,
):
    step = pl.program_id(0)

    @pl.when(step == 0)
    def _():
        for ref in (accq, acck, accv, accp, bq_ref, bv_ref):
            ref[...] = jnp.zeros_like(ref)

    low = h_ref[0]
    accp[...] += inner_rows(o_ref[0], low)
    grad_mixed = times_transpose(low, wp[...]).astype(BF16)
    normed = a_ref[0]
    query, keys, values = q_ref[0], k_ref[0], v_ref[0]
    score_scale = HEAD_DIM**-0.5
    dq, dk, dv = [], [], []
    for head in range(query.shape[1] // HEAD_DIM):
        span = slice(head * HEAD_DIM, (head + 1) * HEAD_DIM)
        qh, kh, vh, gh = query[:, span], keys[:, span], values[:, span], grad_mixed[:, span]
        probs = soft_probs(qh, kh, length)
        dv.append(inner_rows(probs.astype(BF16), gh))
        grad_probs = times_transpose(gh, vh)
        total = jnp.sum(probs * grad_probs, axis=-1, keepdims=True)
        grad_scores = (probs * (grad_probs - total)).astype(BF16)
        dq.append(matmul(grad_scores, kh) * score_scale)
        dk.append(inner_rows(grad_scores, qh) * score_scale)
    dq = jnp.concatenate(dq, axis=1).astype(BF16)
    dk = jnp.concatenate(dk, axis=1).astype(BF16)
    dv = jnp.concatenate(dv, axis=1).astype(BF16)
    bq_ref[...] += jnp.sum(dq.astype(F32), axis=0, keepdims=True)
    bv_ref[...] += jnp.sum(dv.astype(F32), axis=0, keepdims=True)
    part_ref[0] = (
        times_transpose(dq, wq[...]) + times_transpose(dk, wk[...]) + times_transpose(dv, wv[...])
    ).astype(BF16)
    accq[...] += inner_rows(normed, dq)
    acck[...] += inner_rows(normed, dk)
    accv[...] += inner_rows(normed, dv)

    @pl.when(step == pl.num_programs(0) - 1)
    def _():
        gq_ref[...] = accq[...].astype(BF16)
        gk_ref[...] = acck[...].astype(BF16)
        gv_ref[...] = accv[...].astype(BF16)
        gp_ref[...] = accp[...].astype(BF16)


def places():
    here = lax.axis_index("tensor")
    return here, here + 1 - 2 * (here % 2), (here + 2) % 4, 3 - here


def greet(near, far):
    barrier = pltpu.get_barrier_semaphore()
    for other in (near, far):
        pl.semaphore_signal(barrier, inc=1, device_id={"tensor": other}, device_id_type=MESH)
    pl.semaphore_wait(barrier, 2)


def send(src, dst, sems, slot, other):
    copy = pltpu.make_async_remote_copy(
        src_ref=src,
        dst_ref=dst,
        send_sem=sems.at[0, slot],
        recv_sem=sems.at[1, slot],
        device_id={"tensor": other},
        device_id_type=MESH,
    )
    copy.start()
    return copy


def reduce_share(part, near_in, out_buf, far_in, sems):
    here, near, far, diag = places()
    first = send(part.at[diag], near_in.at[0], sems, 0, near)
    second = send(part.at[near], near_in.at[1], sems, 1, near)
    first.wait_recv()
    out_buf[...] = (part[far].astype(F32) + near_in[0].astype(F32)).astype(BF16)
    third = send(out_buf, far_in, sems, 2, far)
    second.wait_recv()
    near_sum = part[here].astype(F32) + near_in[1].astype(F32)
    third.wait_recv()
    total = near_sum + far_in[...].astype(F32)
    first.wait_send()
    second.wait_send()
    third.wait_send()
    return total


def gather_share(out, sems):
    here, near, far, diag = places()
    first = send(out.at[here], out.at[here], sems, 3, far)
    second = send(out.at[here], out.at[here], sems, 4, near)
    first.wait_recv()
    third = send(out.at[far], out.at[far], sems, 5, near)
    second.wait_recv()
    third.wait_recv()
    first.wait_send()
    second.wait_send()
    third.wait_send()


def middle_kernel(part, x_ref, bias, gain, shift, out, h_ref, near_in, out_buf, far_in, sems):
    here, near, far, _ = places()
    greet(near, far)
    total = reduce_share(part, near_in, out_buf, far_in, sems)
    resid = x_ref[here].astype(F32) + total + bias[...]
    h_ref[...] = resid
    hat, _ = normalize(resid)
    out[here] = (hat * gain[...] + shift[...]).astype(BF16)
    gather_share(out, sems)


def turn_kernel(
    part, h_ref, g_ref, bias, gain, out, dh_ref, small, near_in, out_buf, far_in, sems
):
    here, near, far, _ = places()
    rows = h_ref.shape[0]
    greet(near, far)
    total = reduce_share(part, near_in, out_buf, far_in, sems)
    resid = h_ref[...]
    grad = total[rows:]
    own = g_ref[here].astype(F32)
    hat, scale = normalize(resid)
    grad_resid = own + norm_back(hat, scale, gain[...], grad)
    dh_ref[...] = grad_resid
    out[here, :rows] = (resid + total[:rows] + bias[...]).astype(BF16)
    out[here, rows:] = grad_resid.astype(BF16)
    small[0:1] = jnp.sum(grad * hat, axis=0, keepdims=True)
    small[1:2] = jnp.sum(grad, axis=0, keepdims=True)
    small[2:3] = jnp.sum(grad_resid, axis=0, keepdims=True)
    small[3:4] = jnp.sum(own, axis=0, keepdims=True)
    small[4:8] = jnp.zeros((4, small.shape[1]), F32)
    gather_share(out, sems)


def last_kernel(
    part, x_ref, dh_ref, gain, small_in, out, small, near_in, out_buf, far_in, sums, got, sems
):
    here, near, far, _ = places()
    greet(near, far)
    total = reduce_share(part, near_in, out_buf, far_in, sems)
    hat, scale = normalize(x_ref[here].astype(F32))
    out[here] = (dh_ref[...] + norm_back(hat, scale, gain[...], total)).astype(BF16)
    sums[0] = small_in[...]
    sums[0, 4:5] = jnp.sum(total * hat, axis=0, keepdims=True)
    sums[0, 5:6] = jnp.sum(total, axis=0, keepdims=True)
    one = send(sums.at[0], got.at[0], sems, 6, near)
    gather_share(out, sems)
    one.wait()
    sums[1] = sums[0] + got[0]
    two = send(sums.at[1], got.at[1], sems, 7, far)
    two.wait()
    small[...] = sums[1] + got[1]


def whole(count):
    return [pl.BlockSpec(memory_space=pltpu.VMEM)] * count


def fixed(shape):
    return pl.BlockSpec(shape, lambda step: (0,) * len(shape))


def each(shape):
    return pl.BlockSpec((1,) + shape[1:], lambda step: (step,) + (0,) * (len(shape) - 1))


def struct(shape, dtype):
    return jax.ShapeDtypeStruct(shape, dtype)


def exchange(kernel, number, name, outs, rows, width, extra, args):
    return pl.pallas_call(
        kernel,
        out_shape=outs,
        in_specs=whole(len(args)),
        out_specs=whole(len(outs)),
        scratch_shapes=[
            pltpu.VMEM((2, rows, width), BF16),
            pltpu.VMEM((rows, width), BF16),
            pltpu.VMEM((rows, width), BF16),
            *extra,
            pltpu.SemaphoreType.DMA((2, 8)),
        ],
        compiler_params=pltpu.CompilerParams(
            collective_id=number, has_side_effects=True, vmem_limit_bytes=VMEM_LIMIT
        ),
        cost_estimate=pl.CostEstimate(
            flops=0, bytes_accessed=50_000_000, transcendentals=0
        ),
        name=name,
    )(*args)


def stepped(kernel, name, steps, args, arg_specs, outs, out_specs, scratch, flops):
    return pl.pallas_call(
        kernel,
        grid=(steps,),
        out_shape=outs,
        in_specs=arg_specs,
        out_specs=out_specs,
        scratch_shapes=scratch,
        compiler_params=pltpu.CompilerParams(vmem_limit_bytes=VMEM_LIMIT),
        cost_estimate=pl.CostEstimate(
            flops=flops, bytes_accessed=20_000_000, transcendentals=0
        ),
        name=name,
    )(*args)


def partners(count, distance):
    return [(i, i ^ distance) for i in range(count)]


def sum_images(array):
    count = lax.axis_size("dp")
    me = lax.axis_index("dp")
    distances = []
    distance = 1
    while distance < count:
        distances.append(distance)
        distance *= 2
    current = array
    for distance in distances:
        half = current.shape[0] // 2
        bit = (me // distance) % 2
        keep = lax.dynamic_slice_in_dim(current, bit * half, half, 0)
        give = lax.dynamic_slice_in_dim(current, (1 - bit) * half, half, 0)
        got = lax.ppermute(give.astype(BF16), "dp", partners(count, distance))
        current = keep.astype(F32) + got.astype(F32)
    current = current.astype(BF16)
    for distance in reversed(distances):
        bit = (me // distance) % 2
        got = lax.ppermute(current, "dp", partners(count, distance))
        current = jnp.where(
            bit == 0,
            jnp.concatenate([current, got], axis=0),
            jnp.concatenate([got, current], axis=0),
        )
    return current


def sum_small(array):
    count = lax.axis_size("dp")
    distance = 1
    while distance < count:
        array = array + lax.ppermute(array, "dp", partners(count, distance))
        distance *= 2
    return array


def shards(
    tokens, ln1_gain, ln1_shift, w_query, b_query, w_key, w_value, b_value, w_proj, b_proj,
    ln2_gain, ln2_shift, w_fc1, b_fc1, w_fc2, b_fc2, cotangent,
):
    images, length, width = tokens.shape
    assert images == lax.axis_size("tensor") == 4
    local = w_query.shape[1]
    hidden = w_fc1.shape[1]
    rows = (length + 15) // 16 * 16
    pad = ((0, 0), (0, rows - length), (0, 0))
    x = jnp.pad(tokens, pad)
    g = jnp.pad(cotangent, pad)
    flat = lambda v: v.reshape(1, v.shape[0])
    full = (images, rows, width)
    thin = (images, rows, local)

    normed, query, keys, values, mixed, part = stepped(
        lambda *refs: attention_kernel(length, *refs), "attention", images,
        (x, flat(ln1_gain), flat(ln1_shift), w_query, flat(b_query), w_key, w_value,
         flat(b_value), w_proj),
        [each(full), fixed((1, width)), fixed((1, width)), fixed((width, local)),
         fixed((1, local)), fixed((width, local)), fixed((width, local)), fixed((1, local)),
         fixed((local, width))],
        [struct(full, BF16)] + [struct(thin, BF16)] * 4 + [struct(full, BF16)],
        [each(full)] + [each(thin)] * 4 + [each(full)],
        [], 2_000_000_000,
    )
    middle, resid = exchange(
        middle_kernel, 0, "middle", [struct(full, BF16), struct((rows, width), F32)], rows, width,
        [], (part, x, flat(b_proj), flat(ln2_gain), flat(ln2_shift)),
    )
    tall = (images, 2 * rows, width)
    part, fc, grad_bfc1 = stepped(
        feed_kernel, "feed", images,
        (middle, g, w_fc1, flat(b_fc1), w_fc2),
        [each(full), each(full), fixed((width, hidden)), fixed((1, hidden)),
         fixed((hidden, width))],
        [struct(tall, BF16), struct((width + hidden, width), BF16), struct((1, hidden), F32)],
        [each(tall), fixed((width + hidden, width)), fixed((1, hidden))],
        [pltpu.VMEM((width, hidden), F32), pltpu.VMEM((hidden, width), F32)], 6_000_000_000,
    )
    fc = sum_images(fc)
    both, grad_resid, small = exchange(
        turn_kernel, 1, "turn",
        [struct(tall, BF16), struct((rows, width), F32), struct((8, width), F32)],
        2 * rows, width, [],
        (part, resid, g, flat(b_fc2), flat(ln2_gain)),
    )
    layer_out = both[:, :length]
    part, gq, gk, gv, gp, bq, bv = stepped(
        lambda *refs: back_kernel(length, *refs), "back", images,
        (both, mixed, normed, query, keys, values, w_proj, w_query, w_key, w_value),
        [pl.BlockSpec((1, rows, width), lambda step: (step, 1, 0)), each(thin), each(full),
         each(thin), each(thin), each(thin), fixed((local, width))]
        + [fixed((width, local))] * 3,
        [struct(full, BF16)] + [struct((width, local), BF16)] * 3
        + [struct((local, width), BF16)] + [struct((1, local), F32)] * 2,
        [each(full)] + [fixed((width, local))] * 3 + [fixed((local, width))]
        + [fixed((1, local))] * 2,
        [pltpu.VMEM((width, local), F32)] * 3 + [pltpu.VMEM((local, width), F32)], 4_000_000_000,
    )
    heads = sum_images(
        jnp.concatenate([gq.reshape(-1, width), gk.reshape(-1, width), gv.reshape(-1, width), gp])
    )
    out, small = exchange(
        last_kernel, 2, "last", [struct(full, BF16), struct((8, width), F32)], rows, width,
        [pltpu.VMEM((2, 8, width), F32), pltpu.VMEM((2, 8, width), F32)],
        (part, x, grad_resid, flat(ln1_gain), small),
    )
    tokens_grad = out[:, :length]
    pack = jnp.concatenate(
        [small[:6].reshape(-1), grad_bfc1.reshape(-1), bq.reshape(-1), bv.reshape(-1)]
    )
    pack = sum_small(pack)
    row = lambda i: pack[i * width : (i + 1) * width]
    tail = 6 * width + hidden
    heads = heads.astype(F32)
    fc = fc.astype(F32)
    square = lambda i: heads[i * local : (i + 1) * local]
    return (
        layer_out,
        tokens_grad,
        row(4),
        row(5),
        square(0).reshape(width, local),
        pack[tail : tail + local],
        square(1).reshape(width, local),
        square(2).reshape(width, local),
        pack[tail + local : tail + 2 * local],
        square(3),
        row(2),
        row(0),
        row(1),
        fc[:width],
        pack[6 * width : tail],
        fc[width:],
        row(3),
    )


def solution(mesh):
    in_specs = (
        P("dp", None, None),
        P(),
        P(),
        P(None, "tensor"),
        P("tensor"),
        P(None, "tensor"),
        P(None, "tensor"),
        P("tensor"),
        P("tensor", None),
        P(),
        P(),
        P(),
        P(None, "tensor"),
        P("tensor"),
        P("tensor", None),
        P(),
        P("dp", None, None),
    )
    out_specs = (
        P("dp", None, None),
        P("dp", None, None),
        P(),
        P(),
        P(None, "tensor"),
        P("tensor"),
        P(None, "tensor"),
        P(None, "tensor"),
        P("tensor"),
        P("tensor", None),
        P(),
        P(),
        P(),
        P(None, "tensor"),
        P("tensor"),
        P("tensor", None),
        P(),
    )
    return jax.shard_map(shards, mesh=mesh, in_specs=in_specs, out_specs=out_specs, check_vma=False)
```

```python
import jax
import jax.numpy as jnp
from jax import lax
from jax.experimental import pallas as pl
from jax.experimental.pallas import tpu as pltpu
from jax.sharding import PartitionSpec as P

HEAD_DIM = 64
EPSILON = 1e-06
BF16 = jnp.bfloat16
F32 = jnp.float32
MESH = pl.DeviceIdType.MESH
VMEM_LIMIT = 56 * 1024 * 1024


def matmul(left, right):
    return jnp.dot(left, right, preferred_element_type=F32)


def inner_rows(left, right):
    return lax.dot_general(left, right, (((0,), (0,)), ((), ())), preferred_element_type=F32)


def times_transpose(left, right):
    return lax.dot_general(left, right, (((1,), (1,)), ((), ())), preferred_element_type=F32)


def normalize(values):
    center = values - jnp.mean(values, axis=-1, keepdims=True)
    scale = lax.rsqrt(jnp.mean(center * center, axis=-1, keepdims=True) + EPSILON)
    return center * scale, scale


def norm_back(hat, scale, gain, grad):
    inner = grad * gain
    return scale * (
        inner
        - jnp.mean(inner, axis=-1, keepdims=True)
        - hat * jnp.mean(inner * hat, axis=-1, keepdims=True)
    )


def soft_probs(query, keys, length):
    scores = times_transpose(query, keys) * (HEAD_DIM**-0.5)
    column = lax.broadcasted_iota(jnp.int32, scores.shape, 1)
    scores = jnp.where(column < length, scores, -1e30)
    raised = jnp.exp(scores - jnp.max(scores, axis=-1, keepdims=True))
    return raised * (1.0 / jnp.sum(raised, axis=-1, keepdims=True))


def attention_kernel(
    length, x_ref, vec, bias, wq, wk, wv, wp, a_ref, q_ref, k_ref, v_ref, o_ref, part_ref
):
    hat, _ = normalize(x_ref[0].astype(F32))
    normed = (hat * vec[0:1] + vec[1:2]).astype(BF16)
    a_ref[0] = normed
    query = (matmul(normed, wq[...]) + bias[0:1]).astype(BF16)
    keys = matmul(normed, wk[...]).astype(BF16)
    values = (matmul(normed, wv[...]) + bias[1:2]).astype(BF16)
    q_ref[0] = query
    k_ref[0] = keys
    v_ref[0] = values
    heads = []
    for head in range(query.shape[1] // HEAD_DIM):
        cols = slice(head * HEAD_DIM, (head + 1) * HEAD_DIM)
        probs = soft_probs(query[:, cols], keys[:, cols], length)
        heads.append(matmul(probs.astype(BF16), values[:, cols]))
    mixed = jnp.concatenate(heads, axis=1).astype(BF16)
    o_ref[0] = mixed
    part_ref[0] = matmul(mixed, wp[...]).astype(BF16)


def feed_kernel(c_ref, g_ref, w1, vec, w2, part_ref, fc_ref, bias_ref, acc1, acc2):
    step = pl.program_id(0)
    rows = c_ref.shape[1]
    width = c_ref.shape[2]

    @pl.when(step == 0)
    def _():
        acc1[...] = jnp.zeros_like(acc1)
        acc2[...] = jnp.zeros_like(acc2)
        bias_ref[...] = jnp.zeros_like(bias_ref)

    middle = c_ref[0]
    grad = g_ref[0]
    hidden = matmul(middle, w1[...]) + vec[6:7]
    cdf = 0.5 * (1.0 + lax.erf(hidden * (0.5**0.5)))
    slope = cdf + hidden * jnp.exp(-0.5 * hidden * hidden) * 0.3989422804014327
    active = (hidden * cdf).astype(BF16)
    grad_hidden = (times_transpose(grad, w2[...]) * slope).astype(BF16)
    part_ref[0, :rows] = matmul(active, w2[...]).astype(BF16)
    part_ref[0, rows:] = times_transpose(grad_hidden, w1[...]).astype(BF16)
    acc2[...] += inner_rows(active, grad)
    acc1[...] += inner_rows(middle, grad_hidden)
    bias_ref[...] += jnp.sum(grad_hidden.astype(F32), axis=0, keepdims=True)

    @pl.when(step == pl.num_programs(0) - 1)
    def _():
        fc_ref[:width] = acc1[...].astype(BF16)
        fc_ref[width:] = acc2[...].astype(BF16)


def back_kernel(
    length, h_ref, o_ref, a_ref, q_ref, k_ref, v_ref, wp, wq, wk, wv,
    part_ref, grads_ref, bias_ref, acc,
):
    step = pl.program_id(0)

    @pl.when(step == 0)
    def _():
        acc[...] = jnp.zeros_like(acc)
        bias_ref[...] = jnp.zeros_like(bias_ref)

    low = h_ref[0]
    acc[3] += inner_rows(o_ref[0], low)
    grad_mixed = times_transpose(low, wp[...]).astype(BF16)
    normed = a_ref[0]
    query, keys, values = q_ref[0], k_ref[0], v_ref[0]
    score_scale = HEAD_DIM**-0.5
    dq, dk, dv = [], [], []
    for head in range(query.shape[1] // HEAD_DIM):
        cols = slice(head * HEAD_DIM, (head + 1) * HEAD_DIM)
        qh, kh, vh, gh = query[:, cols], keys[:, cols], values[:, cols], grad_mixed[:, cols]
        probs = soft_probs(qh, kh, length)
        dv.append(inner_rows(probs.astype(BF16), gh))
        grad_probs = times_transpose(gh, vh)
        total = jnp.sum(probs * grad_probs, axis=-1, keepdims=True)
        grad_scores = (probs * (grad_probs - total)).astype(BF16)
        dq.append(matmul(grad_scores, kh) * score_scale)
        dk.append(inner_rows(grad_scores, qh) * score_scale)
    dq = jnp.concatenate(dq, axis=1).astype(BF16)
    dk = jnp.concatenate(dk, axis=1).astype(BF16)
    dv = jnp.concatenate(dv, axis=1).astype(BF16)
    bias_ref[0:1] += jnp.sum(dq.astype(F32), axis=0, keepdims=True)
    bias_ref[1:2] += jnp.sum(dv.astype(F32), axis=0, keepdims=True)
    part_ref[0] = (
        times_transpose(dq, wq[...]) + times_transpose(dk, wk[...]) + times_transpose(dv, wv[...])
    ).astype(BF16)
    acc[0] += inner_rows(dq, normed)
    acc[1] += inner_rows(dk, normed)
    acc[2] += inner_rows(dv, normed)

    @pl.when(step == pl.num_programs(0) - 1)
    def _():
        local = acc.shape[1]
        for index in range(4):
            grads_ref[index * local : (index + 1) * local] = acc[index].astype(BF16)


def places():
    here = lax.axis_index("tensor")
    return here, here + 1 - 2 * (here % 2), (here + 2) % 4, 3 - here


def mirror(distance):
    me = lax.axis_index("dp")
    return me + distance - 2 * distance * ((me // distance) % 2)


def greet(others):
    barrier = pltpu.get_barrier_semaphore()
    for other in others:
        pl.semaphore_signal(barrier, inc=1, device_id=other, device_id_type=MESH)
    pl.semaphore_wait(barrier, len(others))


class Sender:
    def __init__(self, sems):
        self.sems = sems
        self.used = 0

    def __call__(self, src, dst, other):
        copy = pltpu.make_async_remote_copy(
            src_ref=src,
            dst_ref=dst,
            send_sem=self.sems.at[0, self.used],
            recv_sem=self.sems.at[1, self.used],
            device_id=other,
            device_id_type=MESH,
        )
        self.used += 1
        copy.start()
        return copy


def take_turns(tasks):
    tasks = list(tasks)
    while tasks:
        for task in list(tasks):
            try:
                next(task)
            except StopIteration:
                tasks.remove(task)


def halvings(first, size, distances):
    steps = []
    offset = first
    for distance in distances:
        half = size // 2
        if half % 16 == 0:
            bit = (lax.axis_index("dp") // distance) % 2
            steps.append((distance, offset + bit * half, offset + (1 - bit) * half, half, True))
            offset = offset + bit * half
            size = half
        else:
            steps.append((distance, offset, offset, size, False))
    return steps


def span(offset, rows):
    return pl.ds(pl.multiple_of(offset, 16), rows)


def sum_down(send, source, work, landing, first, steps):
    at = first
    for distance, kept, given, rows, _ in steps:
        slot = pl.ds(at, rows)
        copy = send(source.at[span(given, rows)], landing.at[slot], {"dp": mirror(distance)})
        yield
        copy.wait()
        mine = source[span(kept, rows)].astype(F32)
        work[span(kept, rows)] = (mine + landing[slot].astype(F32)).astype(BF16)
        source = work
        at += rows


def spread_up(send, work, steps):
    for distance, kept, _, rows, halved in reversed(steps):
        if halved:
            region = work.at[span(kept, rows)]
            copy = send(region, region, {"dp": mirror(distance)})
            yield
            copy.wait()


def sum_all(send, source, work, result, landing, first, steps):
    yield from sum_down(send, source, work, landing, first, steps)
    _, kept, _, rows, _ = steps[-1]
    result[span(kept, rows)] = work[span(kept, rows)]
    yield from spread_up(send, result, steps)


def landing_rows(size, distances):
    return sum(rows for _, _, _, rows, _ in halvings(0, size, distances))


def reduce_share(send, part, near_in, out_buf, far_in):
    here, near, far, diag = places()
    first = send(part.at[diag], near_in.at[0], {"tensor": near})
    second = send(part.at[near], near_in.at[1], {"tensor": near})
    yield
    first.wait_recv()
    out_buf[...] = (part[far].astype(F32) + near_in[0].astype(F32)).astype(BF16)
    third = send(out_buf, far_in, {"tensor": far})
    yield
    second.wait_recv()
    near_sum = part[here].astype(F32) + near_in[1].astype(F32)
    third.wait_recv()
    total = near_sum + far_in[...].astype(F32)
    first.wait_send()
    second.wait_send()
    third.wait_send()
    return total


def gather_share(send, out):
    here, near, far, diag = places()
    first = send(out.at[here], out.at[here], {"tensor": far})
    second = send(out.at[here], out.at[here], {"tensor": near})
    yield
    first.wait_recv()
    third = send(out.at[far], out.at[far], {"tensor": near})
    yield
    second.wait_recv()
    third.wait_recv()
    first.wait_send()
    second.wait_send()
    third.wait_send()


def tensor_others():
    _, near, far, _ = places()
    return [{"tensor": near}, {"tensor": far}]


def dp_orders(count):
    distances = [1 << i for i in range(count.bit_length() - 1)]
    return distances, distances[1:] + distances[:1]


def middle_kernel(part, x_ref, vec, out, h_ref, near_in, out_buf, far_in, sems):
    here, near, far, _ = places()
    send = Sender(sems)
    greet(tensor_others())

    def task():
        total = yield from reduce_share(send, part, near_in, out_buf, far_in)
        resid = x_ref[here].astype(F32) + total + vec[2:3]
        h_ref[...] = resid
        hat, _ = normalize(resid)
        out[here] = (hat * vec[3:4] + vec[4:5]).astype(BF16)
        yield from gather_share(send, out)

    take_turns([task()])


def turn_kernel(
    count, part, h_ref, g_ref, vec, fc, out, dh_ref, small, work,
    near_in, out_buf, far_in, sems, landing,
):
    here = lax.axis_index("tensor")
    rows = h_ref.shape[0]
    send = Sender(sems)
    one, two = dp_orders(count)
    greet(tensor_others() + [{"dp": mirror(d)} for d in one])
    half = fc.shape[0] // 2

    def task():
        total = yield from reduce_share(send, part, near_in, out_buf, far_in)
        resid = h_ref[...]
        grad = total[rows:]
        own = g_ref[here].astype(F32)
        hat, scale = normalize(resid)
        grad_resid = own + norm_back(hat, scale, vec[3:4], grad)
        dh_ref[...] = grad_resid
        out[here, :rows] = (resid + total[:rows] + vec[5:6]).astype(BF16)
        out[here, rows:] = grad_resid.astype(BF16)
        small[0:1] = jnp.sum(grad * hat, axis=0, keepdims=True)
        small[1:2] = jnp.sum(grad, axis=0, keepdims=True)
        small[2:3] = jnp.sum(grad_resid, axis=0, keepdims=True)
        small[3:4] = jnp.sum(own, axis=0, keepdims=True)
        small[4:8] = jnp.zeros((4, small.shape[1]), F32)
        yield from gather_share(send, out)

    take_turns([
        task(),
        sum_down(send, fc, work, landing, 0, halvings(0, half, one)),
        sum_down(send, fc, work, landing, landing_rows(half, one), halvings(half, half, two)),
    ])


def last_kernel(
    count, part, x_ref, dh_ref, vec, small_in, bfc1, bqv, fc, heads,
    out, small, fc_out, heads_out,
    near_in, out_buf, far_in, sems, work, landing, sums, got,
):
    here, near, far, _ = places()
    send = Sender(sems)
    one, two = dp_orders(count)
    greet(tensor_others() + [{"dp": mirror(d)} for d in one])
    fc_half = fc.shape[0] // 2
    half = heads.shape[0] // 2
    local = bqv.shape[1]
    fc_steps = halvings(0, fc_half, one), halvings(fc_half, fc_half, two)
    for steps in fc_steps:
        _, kept, _, rows, _ = steps[-1]
        fc_out[span(kept, rows)] = fc[span(kept, rows)]

    def task():
        total = yield from reduce_share(send, part, near_in, out_buf, far_in)
        hat, scale = normalize(x_ref[here].astype(F32))
        out[here] = (dh_ref[...] + norm_back(hat, scale, vec[0:1], total)).astype(BF16)
        sums[0, :8] = small_in[...]
        sums[0, 4:5] = jnp.sum(total * hat, axis=0, keepdims=True)
        sums[0, 5:6] = jnp.sum(total, axis=0, keepdims=True)
        copy = send(sums.at[0], got.at[0], {"tensor": near})
        yield from gather_share(send, out)
        copy.wait()
        sums[1] = sums[0] + got[0]
        copy = send(sums.at[1], got.at[1], {"tensor": far})
        yield
        copy.wait()
        sums[2] = sums[1] + got[1]
        sums[2, 8:9] = bfc1[...]
        sums[2, 9:11, :local] = bqv[...]
        for slot, distance in enumerate(one, 2):
            copy = send(sums.at[slot], got.at[slot], {"dp": mirror(distance)})
            yield
            copy.wait()
            sums[slot + 1] = sums[slot] + got[slot]
        small[...] = sums[len(one) + 2]

    sums[0, 8:16] = jnp.zeros((8, sums.shape[2]), F32)
    take_turns([
        task(),
        spread_up(send, fc_out, fc_steps[0]),
        spread_up(send, fc_out, fc_steps[1]),
        sum_all(send, heads, work, heads_out, landing, 0, halvings(0, half, one)),
        sum_all(
            send, heads, work, heads_out, landing, landing_rows(half, one),
            halvings(half, half, two),
        ),
    ])


def whole(count):
    return [pl.BlockSpec(memory_space=pltpu.VMEM)] * count


def fixed(shape):
    return pl.BlockSpec(shape, lambda step: (0,) * len(shape))


def each(shape):
    return pl.BlockSpec((1,) + shape[1:], lambda step: (step,) + (0,) * (len(shape) - 1))


def struct(shape, dtype):
    return jax.ShapeDtypeStruct(shape, dtype)


def exchange(kernel, number, name, outs, rows, width, extra, args):
    return pl.pallas_call(
        kernel,
        out_shape=outs,
        in_specs=whole(len(args)),
        out_specs=whole(len(outs)),
        scratch_shapes=[
            pltpu.VMEM((2, rows, width), BF16),
            pltpu.VMEM((rows, width), BF16),
            pltpu.VMEM((rows, width), BF16),
            pltpu.SemaphoreType.DMA((2, 64)),
            *extra,
        ],
        compiler_params=pltpu.CompilerParams(
            collective_id=number, has_side_effects=True, vmem_limit_bytes=VMEM_LIMIT
        ),
        cost_estimate=pl.CostEstimate(
            flops=0, bytes_accessed=50_000_000, transcendentals=0
        ),
        name=name,
    )(*args)


def stepped(kernel, name, steps, args, arg_specs, outs, out_specs, scratch, flops):
    return pl.pallas_call(
        kernel,
        grid=(steps,),
        out_shape=outs,
        in_specs=arg_specs,
        out_specs=out_specs,
        scratch_shapes=scratch,
        compiler_params=pltpu.CompilerParams(vmem_limit_bytes=VMEM_LIMIT),
        cost_estimate=pl.CostEstimate(
            flops=flops, bytes_accessed=20_000_000, transcendentals=0
        ),
        name=name,
    )(*args)


def shards(
    tokens, ln1_gain, ln1_shift, w_query, b_query, w_key, w_value, b_value, w_proj, b_proj,
    ln2_gain, ln2_shift, w_fc1, b_fc1, w_fc2, b_fc2, cotangent,
):
    images, length, width = tokens.shape
    assert images == lax.axis_size("tensor") == 4
    local = w_query.shape[1]
    hidden = w_fc1.shape[1]
    rows = (length + 15) // 16 * 16
    pad = ((0, 0), (0, rows - length), (0, 0))
    x = jnp.pad(tokens, pad)
    g = jnp.pad(cotangent, pad)
    full = (images, rows, width)
    thin = (images, rows, local)
    tall = (images, 2 * rows, width)
    count = lax.axis_size("dp")
    one, two = dp_orders(count)
    assert hidden == width and 4 * local == width and 1 << len(one) == count
    vec = jnp.stack([ln1_gain, ln1_shift, b_proj, ln2_gain, ln2_shift, b_fc2, b_fc1])
    bias = jnp.stack([b_query, b_value])

    normed, query, keys, values, mixed, part = stepped(
        lambda *refs: attention_kernel(length, *refs), "attention", images,
        (x, vec, bias, w_query, w_key, w_value, w_proj),
        [each(full), fixed(vec.shape), fixed(bias.shape)]
        + [fixed((width, local))] * 3 + [fixed((local, width))],
        [struct(full, BF16)] + [struct(thin, BF16)] * 4 + [struct(full, BF16)],
        [each(full)] + [each(thin)] * 4 + [each(full)],
        [], 2_000_000_000,
    )
    middle, resid = exchange(
        middle_kernel, 0, "middle", [struct(full, BF16), struct((rows, width), F32)], rows, width,
        [], (part, x, vec),
    )
    part, fc, grad_bfc1 = stepped(
        feed_kernel, "feed", images,
        (middle, g, w_fc1, vec, w_fc2),
        [each(full), each(full), fixed((width, hidden)), fixed(vec.shape),
         fixed((hidden, width))],
        [struct(tall, BF16), struct((width + hidden, width), BF16), struct((1, hidden), F32)],
        [each(tall), fixed((width + hidden, width)), fixed((1, hidden))],
        [pltpu.VMEM((width, hidden), F32), pltpu.VMEM((hidden, width), F32)], 6_000_000_000,
    )
    fc_land = landing_rows(width, one) + landing_rows(width, two)
    both, grad_resid, small, fc = exchange(
        lambda *refs: turn_kernel(count, *refs), 1, "turn",
        [struct(tall, BF16), struct((rows, width), F32), struct((8, width), F32),
         struct(fc.shape, BF16)],
        2 * rows, width, [pltpu.VMEM((fc_land, width), BF16)],
        (part, resid, g, vec, fc),
    )
    layer_out = both[:, :length]
    part, heads, grad_bias = stepped(
        lambda *refs: back_kernel(length, *refs), "back", images,
        (both, mixed, normed, query, keys, values, w_proj, w_query, w_key, w_value),
        [pl.BlockSpec((1, rows, width), lambda step: (step, 1, 0)), each(thin), each(full),
         each(thin), each(thin), each(thin), fixed((local, width))]
        + [fixed((width, local))] * 3,
        [struct(full, BF16), struct((width, width), BF16), struct((2, local), F32)],
        [each(full), fixed((width, width)), fixed((2, local))],
        [pltpu.VMEM((4, local, width), F32)], 4_000_000_000,
    )
    heads_land = landing_rows(width // 2, one) + landing_rows(width // 2, two)
    out, small, fc, heads = exchange(
        lambda *refs: last_kernel(count, *refs), 2, "last",
        [struct(full, BF16), struct((16, width), F32), struct(fc.shape, BF16),
         struct(heads.shape, BF16)],
        rows, width,
        [pltpu.VMEM(heads.shape, BF16), pltpu.VMEM((heads_land, width), BF16),
         pltpu.VMEM((3 + len(one), 16, width), F32),
         pltpu.VMEM((2 + len(one), 16, width), F32)],
        (part, x, grad_resid, vec, small, grad_bfc1, grad_bias, fc, heads),
    )
    tokens_grad = out[:, :length]
    heads = heads.astype(F32)
    fc = fc.astype(F32)
    square = lambda i: heads[i * local : (i + 1) * local]
    return (
        layer_out,
        tokens_grad,
        small[4],
        small[5],
        square(0).T,
        small[9, :local],
        square(1).T,
        square(2).T,
        small[10, :local],
        square(3),
        small[2],
        small[0],
        small[1],
        fc[:width],
        small[8, :hidden],
        fc[width:],
        small[3],
    )


def solution(mesh):
    in_specs = (
        P("dp", None, None),
        P(),
        P(),
        P(None, "tensor"),
        P("tensor"),
        P(None, "tensor"),
        P(None, "tensor"),
        P("tensor"),
        P("tensor", None),
        P(),
        P(),
        P(),
        P(None, "tensor"),
        P("tensor"),
        P("tensor", None),
        P(),
        P("dp", None, None),
    )
    out_specs = (
        P("dp", None, None),
        P("dp", None, None),
        P(),
        P(),
        P(None, "tensor"),
        P("tensor"),
        P(None, "tensor"),
        P(None, "tensor"),
        P("tensor"),
        P("tensor", None),
        P(),
        P(),
        P(),
        P(None, "tensor"),
        P("tensor"),
        P("tensor", None),
        P(),
    )
    return jax.shard_map(shards, mesh=mesh, in_specs=in_specs, out_specs=out_specs, check_vma=False)
```

```python
import jax
import jax.numpy as jnp
from jax import lax
from jax.experimental import pallas as pl
from jax.experimental.pallas import tpu as pltpu
from jax.sharding import PartitionSpec as P

HEAD_DIM = 64
EPSILON = 1e-06
BF16 = jnp.bfloat16
F32 = jnp.float32
MESH = pl.DeviceIdType.MESH
VMEM_LIMIT = 56 * 1024 * 1024


def matmul(left, right):
    return jnp.dot(left, right, preferred_element_type=F32)


def inner_rows(left, right):
    return lax.dot_general(left, right, (((0,), (0,)), ((), ())), preferred_element_type=F32)


def times_transpose(left, right):
    return lax.dot_general(left, right, (((1,), (1,)), ((), ())), preferred_element_type=F32)


def normalize(values):
    center = values - jnp.mean(values, axis=-1, keepdims=True)
    scale = lax.rsqrt(jnp.mean(center * center, axis=-1, keepdims=True) + EPSILON)
    return center * scale, scale


def norm_back(hat, scale, gain, grad):
    inner = grad * gain
    return scale * (
        inner
        - jnp.mean(inner, axis=-1, keepdims=True)
        - hat * jnp.mean(inner * hat, axis=-1, keepdims=True)
    )


def line(ref):
    return ref[...].reshape(1, ref.shape[0])


def soft_probs(query, keys, length):
    scores = times_transpose(query, keys) * (HEAD_DIM**-0.5)
    column = lax.broadcasted_iota(jnp.int32, scores.shape, 1)
    scores = jnp.where(column < length, scores, -1e30)
    raised = jnp.exp(scores - jnp.max(scores, axis=-1, keepdims=True))
    return raised * (1.0 / jnp.sum(raised, axis=-1, keepdims=True))


def attention_kernel(
    length, x_ref, gain, shift, bq, bv, wq, wk, wv, wp, a_ref, q_ref, k_ref, v_ref, o_ref, part_ref
):
    hat, _ = normalize(x_ref[0].astype(F32))
    normed = (hat * line(gain) + line(shift)).astype(BF16)
    a_ref[0] = normed
    query = (times_transpose(normed, wq[...]) + line(bq)).astype(BF16)
    keys = times_transpose(normed, wk[...]).astype(BF16)
    values = (times_transpose(normed, wv[...]) + line(bv)).astype(BF16)
    q_ref[0] = query
    k_ref[0] = keys
    v_ref[0] = values
    heads = []
    for head in range(query.shape[1] // HEAD_DIM):
        cols = slice(head * HEAD_DIM, (head + 1) * HEAD_DIM)
        probs = soft_probs(query[:, cols], keys[:, cols], length)
        heads.append(matmul(probs.astype(BF16), values[:, cols]))
    mixed = jnp.concatenate(heads, axis=1).astype(BF16)
    o_ref[0] = mixed
    part_ref[0] = matmul(mixed, wp[...]).astype(BF16)


def feed_kernel(c_ref, g_ref, w1, b1, w2, part_ref, fc_ref, bias_ref, acc1, acc2):
    step = pl.program_id(0)
    rows = c_ref.shape[1]
    width = c_ref.shape[2]

    @pl.when(step == 0)
    def _():
        acc1[...] = jnp.zeros_like(acc1)
        acc2[...] = jnp.zeros_like(acc2)
        bias_ref[...] = jnp.zeros_like(bias_ref)

    middle = c_ref[0]
    grad = g_ref[0]
    hidden = matmul(middle, w1[...]) + line(b1)
    cdf = 0.5 * (1.0 + lax.erf(hidden * (0.5**0.5)))
    slope = cdf + hidden * jnp.exp(-0.5 * hidden * hidden) * 0.3989422804014327
    active = (hidden * cdf).astype(BF16)
    grad_hidden = (times_transpose(grad, w2[...]) * slope).astype(BF16)
    part_ref[0, :rows] = matmul(active, w2[...]).astype(BF16)
    part_ref[0, rows:] = times_transpose(grad_hidden, w1[...]).astype(BF16)
    acc2[...] += inner_rows(active, grad)
    acc1[...] += inner_rows(middle, grad_hidden)
    bias_ref[...] += jnp.sum(grad_hidden.astype(F32), axis=0, keepdims=True)

    @pl.when(step == pl.num_programs(0) - 1)
    def _():
        fc_ref[:width] = acc1[...].astype(BF16)
        fc_ref[width:] = acc2[...].astype(BF16)


def image_back(
    length, image, start, h_ref, o_ref, a_ref, q_ref, k_ref, v_ref, wp, wq, wk, wv,
    part_ref, bias_ref, acc,
):
    def add(ref, index, value):
        ref[index] = value if start else ref[index] + value

    rows = a_ref.shape[1]
    low = h_ref[image, rows:]
    add(acc, 3, inner_rows(o_ref[image], low))
    grad_mixed = times_transpose(low, wp[...]).astype(BF16)
    normed = a_ref[image]
    query, keys, values = q_ref[image], k_ref[image], v_ref[image]
    score_scale = HEAD_DIM**-0.5
    dq, dk, dv = [], [], []
    for head in range(query.shape[1] // HEAD_DIM):
        cols = slice(head * HEAD_DIM, (head + 1) * HEAD_DIM)
        qh, kh, vh, gh = query[:, cols], keys[:, cols], values[:, cols], grad_mixed[:, cols]
        probs = soft_probs(qh, kh, length)
        dv.append(inner_rows(probs.astype(BF16), gh))
        grad_probs = times_transpose(gh, vh)
        total = jnp.sum(probs * grad_probs, axis=-1, keepdims=True)
        grad_scores = (probs * (grad_probs - total)).astype(BF16)
        dq.append(matmul(grad_scores, kh) * score_scale)
        dk.append(inner_rows(grad_scores, qh) * score_scale)
    dq = jnp.concatenate(dq, axis=1).astype(BF16)
    dk = jnp.concatenate(dk, axis=1).astype(BF16)
    dv = jnp.concatenate(dv, axis=1).astype(BF16)
    add(bias_ref, slice(0, 1), jnp.sum(dq.astype(F32), axis=0, keepdims=True))
    add(bias_ref, slice(1, 2), jnp.sum(dv.astype(F32), axis=0, keepdims=True))
    part_ref[image] = (
        matmul(dq, wq[...]) + matmul(dk, wk[...]) + matmul(dv, wv[...])
    ).astype(BF16)
    add(acc, 0, inner_rows(dq, normed))
    add(acc, 1, inner_rows(dk, normed))
    add(acc, 2, inner_rows(dv, normed))


def places():
    here = lax.axis_index("tensor")
    return here, here + 1 - 2 * (here % 2), (here + 2) % 4, 3 - here


def mirror(distance):
    me = lax.axis_index("dp")
    return me + distance - 2 * distance * ((me // distance) % 2)


def greet(others):
    barrier = pltpu.get_barrier_semaphore()
    for other in others:
        pl.semaphore_signal(barrier, inc=1, device_id=other, device_id_type=MESH)
    pl.semaphore_wait(barrier, len(others))


class Sender:
    def __init__(self, sems):
        self.sems = sems
        self.used = 0

    def __call__(self, src, dst, other):
        copy = pltpu.make_async_remote_copy(
            src_ref=src,
            dst_ref=dst,
            send_sem=self.sems.at[0, self.used],
            recv_sem=self.sems.at[1, self.used],
            device_id=other,
            device_id_type=MESH,
        )
        self.used += 1
        copy.start()
        return copy


def take_turns(tasks):
    tasks = list(tasks)
    while tasks:
        for task in list(tasks):
            try:
                next(task)
            except StopIteration:
                tasks.remove(task)


def halvings(first, size, distances):
    steps = []
    offset = first
    for distance in distances:
        half = size // 2
        if half % 16 == 0:
            bit = (lax.axis_index("dp") // distance) % 2
            steps.append((distance, offset + bit * half, offset + (1 - bit) * half, half, True))
            offset = offset + bit * half
            size = half
        else:
            steps.append((distance, offset, offset, size, False))
    return steps


def span(offset, rows):
    return pl.ds(pl.multiple_of(offset, 16), rows)


def sum_down(send, source, work, landing, first, steps):
    at = first
    for distance, kept, given, rows, _ in steps:
        slot = pl.ds(at, rows)
        copy = send(source.at[span(given, rows)], landing.at[slot], {"dp": mirror(distance)})
        yield
        copy.wait()
        mine = source[span(kept, rows)].astype(F32)
        work[span(kept, rows)] = (mine + landing[slot].astype(F32)).astype(BF16)
        source = work
        at += rows


def spread_up(send, work, steps):
    for distance, kept, _, rows, halved in reversed(steps):
        if halved:
            region = work.at[span(kept, rows)]
            copy = send(region, region, {"dp": mirror(distance)})
            yield
            copy.wait()


def sum_all(send, source, work, result, landing, first, steps):
    yield from sum_down(send, source, work, landing, first, steps)
    _, kept, _, rows, _ = steps[-1]
    result[span(kept, rows)] = work[span(kept, rows)]
    yield from spread_up(send, result, steps)


def reduce_share(send, part, near_in, out_buf, far_in, prepare=None):
    here, near, far, diag = places()
    ready = prepare or (lambda image, start: None)
    ready(diag, True)
    first = send(part.at[diag], near_in.at[0], {"tensor": near})
    ready(near, False)
    second = send(part.at[near], near_in.at[1], {"tensor": near})
    yield
    ready(far, False)
    first.wait_recv()
    out_buf[...] = (part[far].astype(F32) + near_in[0].astype(F32)).astype(BF16)
    third = send(out_buf, far_in, {"tensor": far})
    ready(here, False)
    yield
    second.wait_recv()
    near_sum = part[here].astype(F32) + near_in[1].astype(F32)
    third.wait_recv()
    total = near_sum + far_in[...].astype(F32)
    first.wait_send()
    second.wait_send()
    third.wait_send()
    return total


def gather_share(send, out):
    here, near, far, diag = places()
    first = send(out.at[here], out.at[here], {"tensor": far})
    second = send(out.at[here], out.at[here], {"tensor": near})
    yield
    first.wait_recv()
    third = send(out.at[far], out.at[far], {"tensor": near})
    yield
    second.wait_recv()
    third.wait_recv()
    first.wait_send()
    second.wait_send()
    third.wait_send()


def tensor_others():
    _, near, far, _ = places()
    return [{"tensor": near}, {"tensor": far}]


def dp_distances(count):
    return [1 << i for i in range(count.bit_length() - 1)]


def streams(rows, count, parts):
    one = dp_distances(count)
    orders = [one, one[1:] + one[:1]]
    size = rows // parts
    found, at = [], 0
    for index in range(parts):
        steps = halvings(index * size, size, orders[index % 2])
        found.append((at, steps))
        at += sum(step[3] for step in steps)
    return found, at


def middle_kernel(part, x_ref, bias, gain, shift, out, h_ref, near_in, out_buf, far_in, sems):
    here, near, far, _ = places()
    send = Sender(sems)
    greet(tensor_others())

    def task():
        total = yield from reduce_share(send, part, near_in, out_buf, far_in)
        resid = x_ref[here].astype(F32) + total + line(bias)
        h_ref[...] = resid
        hat, _ = normalize(resid)
        out[here] = (hat * line(gain) + line(shift)).astype(BF16)
        yield from gather_share(send, out)

    take_turns([task()])


def turn_kernel(
    count, part, h_ref, g_ref, bias, gain, fc, out, dh_ref, small, work,
    near_in, out_buf, far_in, sems, landing,
):
    here = lax.axis_index("tensor")
    rows = h_ref.shape[0]
    send = Sender(sems)
    greet(tensor_others() + [{"dp": mirror(d)} for d in dp_distances(count)])
    found, _ = streams(fc.shape[0], count, 4)

    def task():
        total = yield from reduce_share(send, part, near_in, out_buf, far_in)
        resid = h_ref[...]
        grad = total[rows:]
        own = g_ref[here].astype(F32)
        hat, scale = normalize(resid)
        grad_resid = own + norm_back(hat, scale, line(gain), grad)
        dh_ref[...] = grad_resid
        out[here, :rows] = (resid + total[:rows] + line(bias)).astype(BF16)
        out[here, rows:] = grad_resid.astype(BF16)
        small[0:1] = jnp.sum(grad * hat, axis=0, keepdims=True)
        small[1:2] = jnp.sum(grad, axis=0, keepdims=True)
        small[2:3] = jnp.sum(grad_resid, axis=0, keepdims=True)
        small[3:4] = jnp.sum(own, axis=0, keepdims=True)
        small[4:8] = jnp.zeros((4, small.shape[1]), F32)
        yield from gather_share(send, out)

    take_turns([
        task(),
        *(sum_down(send, fc, work, landing, at, steps) for at, steps in found),
    ])


def last_kernel(
    count, length, both, mixed, normed, query, keys, values, wp, wq, wk, wv,
    x_ref, dh_ref, gain, small_in, bfc1, fc,
    out, small, fc_out, heads_out,
    near_in, out_buf, far_in, sems, part, acc, bias, heads, work, landing, sums, got,
):
    here, near, far, _ = places()
    send = Sender(sems)
    distances = dp_distances(count)
    greet(tensor_others() + [{"dp": mirror(d)} for d in distances])
    local = wp.shape[0]
    fc_streams, _ = streams(fc.shape[0], count, 4)
    head_streams, _ = streams(heads.shape[0], count, 2)
    for _, steps in fc_streams:
        _, kept, _, rows, _ = steps[-1]
        fc_out[span(kept, rows)] = fc[span(kept, rows)]
    sums[0, 8:16] = jnp.zeros((8, sums.shape[2]), F32)

    def prepare(image, start):
        image_back(
            length, image, start, both, mixed, normed, query, keys, values,
            wp, wq, wk, wv, part, bias, acc,
        )

    def task():
        total = yield from reduce_share(send, part, near_in, out_buf, far_in, prepare)
        hat, scale = normalize(x_ref[here].astype(F32))
        out[here] = (dh_ref[...] + norm_back(hat, scale, line(gain), total)).astype(BF16)
        sums[0, :8] = small_in[...]
        sums[0, 4:5] = jnp.sum(total * hat, axis=0, keepdims=True)
        sums[0, 5:6] = jnp.sum(total, axis=0, keepdims=True)
        copy = send(sums.at[0], got.at[0], {"tensor": near})
        yield from gather_share(send, out)
        copy.wait()
        sums[1] = sums[0] + got[0]
        copy = send(sums.at[1], got.at[1], {"tensor": far})
        yield
        copy.wait()
        sums[2] = sums[1] + got[1]
        sums[2, 8:9] = bfc1[...]
        sums[2, 9:11, :local] = bias[...]
        for slot, distance in enumerate(distances, 2):
            copy = send(sums.at[slot], got.at[slot], {"dp": mirror(distance)})
            yield
            copy.wait()
            sums[slot + 1] = sums[slot] + got[slot]
        small[...] = sums[len(distances) + 2]

    def head_task(index, at, steps):
        yield
        if index == 0:
            for block in range(4):
                heads[block * local : (block + 1) * local] = acc[block].astype(BF16)
        yield from sum_all(send, heads, work, heads_out, landing, at, steps)

    take_turns([
        *(spread_up(send, fc_out, steps) for _, steps in fc_streams),
        task(),
        *(head_task(i, at, steps) for i, (at, steps) in enumerate(head_streams)),
    ])


def whole(count):
    return [pl.BlockSpec(memory_space=pltpu.VMEM)] * count


def fixed(shape):
    return pl.BlockSpec(shape, lambda step: (0,) * len(shape))


def each(shape):
    return pl.BlockSpec((1,) + shape[1:], lambda step: (step,) + (0,) * (len(shape) - 1))


def struct(shape, dtype):
    return jax.ShapeDtypeStruct(shape, dtype)


def exchange(kernel, number, name, outs, rows, width, extra, args):
    return pl.pallas_call(
        kernel,
        out_shape=outs,
        in_specs=whole(len(args)),
        out_specs=whole(len(outs)),
        scratch_shapes=[
            pltpu.VMEM((2, rows, width), BF16),
            pltpu.VMEM((rows, width), BF16),
            pltpu.VMEM((rows, width), BF16),
            pltpu.SemaphoreType.DMA((2, 64)),
            *extra,
        ],
        compiler_params=pltpu.CompilerParams(
            collective_id=number, has_side_effects=True, vmem_limit_bytes=VMEM_LIMIT
        ),
        cost_estimate=pl.CostEstimate(
            flops=0, bytes_accessed=50_000_000, transcendentals=0
        ),
        name=name,
    )(*args)


def stepped(kernel, name, steps, args, arg_specs, outs, out_specs, scratch, flops):
    return pl.pallas_call(
        kernel,
        grid=(steps,),
        out_shape=outs,
        in_specs=arg_specs,
        out_specs=out_specs,
        scratch_shapes=scratch,
        compiler_params=pltpu.CompilerParams(vmem_limit_bytes=VMEM_LIMIT),
        cost_estimate=pl.CostEstimate(
            flops=flops, bytes_accessed=20_000_000, transcendentals=0
        ),
        name=name,
    )(*args)


def shards(
    tokens, ln1_gain, ln1_shift, w_query, b_query, w_key, w_value, b_value, w_proj, b_proj,
    ln2_gain, ln2_shift, w_fc1, b_fc1, w_fc2, b_fc2, cotangent,
):
    images, length, width = tokens.shape
    assert images == lax.axis_size("tensor") == 4
    local = w_query.shape[1]
    hidden = w_fc1.shape[1]
    rows = (length + 15) // 16 * 16
    pad = ((0, 0), (0, rows - length), (0, 0))
    x = jnp.pad(tokens, pad)
    g = jnp.pad(cotangent, pad)
    full = (images, rows, width)
    thin = (images, rows, local)
    tall = (images, 2 * rows, width)
    count = lax.axis_size("dp")
    distances = dp_distances(count)
    assert hidden == width and 4 * local == width and 1 << len(distances) == count
    turned = [weight.T for weight in (w_query, w_key, w_value)]

    normed, query, keys, values, mixed, part = stepped(
        lambda *refs: attention_kernel(length, *refs), "attention", images,
        (x, ln1_gain, ln1_shift, b_query, b_value, *turned, w_proj),
        [each(full)] + [fixed((width,))] * 2 + [fixed((local,))] * 2
        + [fixed((local, width))] * 4,
        [struct(full, BF16)] + [struct(thin, BF16)] * 4 + [struct(full, BF16)],
        [each(full)] + [each(thin)] * 4 + [each(full)],
        [], 2_000_000_000,
    )
    middle, resid = exchange(
        middle_kernel, 0, "middle", [struct(full, BF16), struct((rows, width), F32)], rows, width,
        [], (part, x, b_proj, ln2_gain, ln2_shift),
    )
    part, fc, grad_bfc1 = stepped(
        feed_kernel, "feed", images,
        (middle, g, w_fc1, b_fc1, w_fc2),
        [each(full), each(full), fixed((width, hidden)), fixed((hidden,)),
         fixed((hidden, width))],
        [struct(tall, BF16), struct((width + hidden, width), BF16), struct((1, hidden), F32)],
        [each(tall), fixed((width + hidden, width)), fixed((1, hidden))],
        [pltpu.VMEM((width, hidden), F32), pltpu.VMEM((hidden, width), F32)], 6_000_000_000,
    )
    _, land = streams(width + hidden, count, 4)
    both, grad_resid, small, fc = exchange(
        lambda *refs: turn_kernel(count, *refs), 1, "turn",
        [struct(tall, BF16), struct((rows, width), F32), struct((8, width), F32),
         struct(fc.shape, BF16)],
        2 * rows, width, [pltpu.VMEM((land, width), BF16)],
        (part, resid, g, b_fc2, ln2_gain, fc),
    )
    layer_out = both[:, :length]
    _, land = streams(width, count, 2)
    out, small, fc, heads = exchange(
        lambda *refs: last_kernel(count, length, *refs), 2, "last",
        [struct(full, BF16), struct((16, width), F32), struct(fc.shape, BF16),
         struct((width, width), BF16)],
        rows, width,
        [pltpu.VMEM(full, BF16), pltpu.VMEM((4, local, width), F32),
         pltpu.VMEM((2, local), F32), pltpu.VMEM((width, width), BF16),
         pltpu.VMEM((width, width), BF16), pltpu.VMEM((land, width), BF16),
         pltpu.VMEM((3 + len(distances), 16, width), F32),
         pltpu.VMEM((2 + len(distances), 16, width), F32)],
        (both, mixed, normed, query, keys, values, w_proj, *turned,
         x, grad_resid, ln1_gain, small, grad_bfc1, fc),
    )
    tokens_grad = out[:, :length]
    heads = heads.astype(F32)
    fc = fc.astype(F32)
    square = lambda i: heads[i * local : (i + 1) * local]
    return (
        layer_out,
        tokens_grad,
        small[4],
        small[5],
        square(0).T,
        small[9, :local],
        square(1).T,
        square(2).T,
        small[10, :local],
        square(3),
        small[2],
        small[0],
        small[1],
        fc[:width],
        small[8, :hidden],
        fc[width:],
        small[3],
    )


def solution(mesh):
    in_specs = (
        P("dp", None, None),
        P(),
        P(),
        P(None, "tensor"),
        P("tensor"),
        P(None, "tensor"),
        P(None, "tensor"),
        P("tensor"),
        P("tensor", None),
        P(),
        P(),
        P(),
        P(None, "tensor"),
        P("tensor"),
        P("tensor", None),
        P(),
        P("dp", None, None),
    )
    out_specs = (
        P("dp", None, None),
        P("dp", None, None),
        P(),
        P(),
        P(None, "tensor"),
        P("tensor"),
        P(None, "tensor"),
        P(None, "tensor"),
        P("tensor"),
        P("tensor", None),
        P(),
        P(),
        P(),
        P(None, "tensor"),
        P("tensor"),
        P("tensor", None),
        P(),
    )
    return jax.shard_map(shards, mesh=mesh, in_specs=in_specs, out_specs=out_specs, check_vma=False)
```

```python
import jax
import jax.numpy as jnp
from jax import lax
from jax.experimental import pallas as pl
from jax.experimental.pallas import tpu as pltpu
from jax.sharding import PartitionSpec as P

HEAD_DIM = 64
EPSILON = 1e-06
BF16 = jnp.bfloat16
F32 = jnp.float32
MESH = pl.DeviceIdType.MESH
VMEM_LIMIT = 56 * 1024 * 1024


def matmul(left, right):
    return jnp.dot(left, right, preferred_element_type=F32)


def inner_rows(left, right):
    return lax.dot_general(left, right, (((0,), (0,)), ((), ())), preferred_element_type=F32)


def times_transpose(left, right):
    return lax.dot_general(left, right, (((1,), (1,)), ((), ())), preferred_element_type=F32)


def normalize(values):
    center = values - jnp.mean(values, axis=-1, keepdims=True)
    scale = lax.rsqrt(jnp.mean(center * center, axis=-1, keepdims=True) + EPSILON)
    return center * scale, scale


def norm_back(hat, scale, gain, grad):
    inner = grad * gain
    return scale * (
        inner
        - jnp.mean(inner, axis=-1, keepdims=True)
        - hat * jnp.mean(inner * hat, axis=-1, keepdims=True)
    )


def line(ref):
    return ref[...].reshape(1, ref.shape[0])


def soft_probs(query, keys, length):
    scores = times_transpose(query, keys) * (HEAD_DIM**-0.5)
    column = lax.broadcasted_iota(jnp.int32, scores.shape, 1)
    scores = jnp.where(column < length, scores, -1e30)
    raised = jnp.exp(scores - jnp.max(scores, axis=-1, keepdims=True))
    return raised * (1.0 / jnp.sum(raised, axis=-1, keepdims=True))


def attention_kernel(
    length, x_ref, gain, shift, bq, bv, wq, wk, wv, wp, a_ref, q_ref, k_ref, v_ref, o_ref, part_ref
):
    hat, _ = normalize(x_ref[0].astype(F32))
    normed = (hat * line(gain) + line(shift)).astype(BF16)
    a_ref[0] = normed
    query = (times_transpose(normed, wq[...]) + line(bq)).astype(BF16)
    keys = times_transpose(normed, wk[...]).astype(BF16)
    values = (times_transpose(normed, wv[...]) + line(bv)).astype(BF16)
    q_ref[0] = query
    k_ref[0] = keys
    v_ref[0] = values
    heads = []
    for head in range(query.shape[1] // HEAD_DIM):
        cols = slice(head * HEAD_DIM, (head + 1) * HEAD_DIM)
        probs = soft_probs(query[:, cols], keys[:, cols], length)
        heads.append(matmul(probs.astype(BF16), values[:, cols]))
    mixed = jnp.concatenate(heads, axis=1).astype(BF16)
    o_ref[0] = mixed
    part_ref[0] = matmul(mixed, wp[...]).astype(BF16)


def feed_kernel(c_ref, g_ref, w1, b1, w2, part_ref, branch_ref, fc_ref, bias_ref, acc1, acc2):
    step = pl.program_id(0)
    width = c_ref.shape[2]

    @pl.when(step == 0)
    def _():
        acc1[...] = jnp.zeros_like(acc1)
        acc2[...] = jnp.zeros_like(acc2)
        bias_ref[...] = jnp.zeros_like(bias_ref)

    middle = c_ref[0]
    grad = g_ref[0]
    hidden = matmul(middle, w1[...]) + line(b1)
    cdf = 0.5 * (1.0 + lax.erf(hidden * (0.5**0.5)))
    slope = cdf + hidden * jnp.exp(-0.5 * hidden * hidden) * 0.3989422804014327
    active = (hidden * cdf).astype(BF16)
    grad_hidden = (times_transpose(grad, w2[...]) * slope).astype(BF16)
    branch_ref[0] = matmul(active, w2[...]).astype(BF16)
    part_ref[0] = times_transpose(grad_hidden, w1[...]).astype(BF16)
    acc2[...] += inner_rows(active, grad)
    acc1[...] += inner_rows(middle, grad_hidden)
    bias_ref[...] += jnp.sum(grad_hidden.astype(F32), axis=0, keepdims=True)

    @pl.when(step == pl.num_programs(0) - 1)
    def _():
        fc_ref[:width] = acc1[...].astype(BF16)
        fc_ref[width:] = acc2[...].astype(BF16)


def image_back(
    length, image, start, h_ref, o_ref, a_ref, q_ref, k_ref, v_ref, wp, wq, wk, wv,
    part_ref, bias_ref, acc,
):
    def add(ref, index, value):
        ref[index] = value if start else ref[index] + value

    low = h_ref[image]
    add(acc, 3, inner_rows(o_ref[image], low))
    grad_mixed = times_transpose(low, wp[...]).astype(BF16)
    normed = a_ref[image]
    query, keys, values = q_ref[image], k_ref[image], v_ref[image]
    score_scale = HEAD_DIM**-0.5
    dq, dk, dv = [], [], []
    for head in range(query.shape[1] // HEAD_DIM):
        cols = slice(head * HEAD_DIM, (head + 1) * HEAD_DIM)
        qh, kh, vh, gh = query[:, cols], keys[:, cols], values[:, cols], grad_mixed[:, cols]
        probs = soft_probs(qh, kh, length)
        dv.append(inner_rows(probs.astype(BF16), gh))
        grad_probs = times_transpose(gh, vh)
        total = jnp.sum(probs * grad_probs, axis=-1, keepdims=True)
        grad_scores = (probs * (grad_probs - total)).astype(BF16)
        dq.append(matmul(grad_scores, kh) * score_scale)
        dk.append(inner_rows(grad_scores, qh) * score_scale)
    dq = jnp.concatenate(dq, axis=1).astype(BF16)
    dk = jnp.concatenate(dk, axis=1).astype(BF16)
    dv = jnp.concatenate(dv, axis=1).astype(BF16)
    add(bias_ref, slice(0, 1), jnp.sum(dq.astype(F32), axis=0, keepdims=True))
    add(bias_ref, slice(1, 2), jnp.sum(dv.astype(F32), axis=0, keepdims=True))
    part_ref[image] = (
        matmul(dq, wq[...]) + matmul(dk, wk[...]) + matmul(dv, wv[...])
    ).astype(BF16)
    add(acc, 0, inner_rows(dq, normed))
    add(acc, 1, inner_rows(dk, normed))
    add(acc, 2, inner_rows(dv, normed))


def places():
    here = lax.axis_index("tensor")
    return here, here + 1 - 2 * (here % 2), (here + 2) % 4, 3 - here


def mirror(distance):
    me = lax.axis_index("dp")
    return me + distance - 2 * distance * ((me // distance) % 2)


def greet(others):
    barrier = pltpu.get_barrier_semaphore()
    for other in others:
        pl.semaphore_signal(barrier, inc=1, device_id=other, device_id_type=MESH)
    pl.semaphore_wait(barrier, len(others))


class Sender:
    def __init__(self, sems):
        self.sems = sems
        self.used = 0

    def __call__(self, src, dst, other):
        copy = pltpu.make_async_remote_copy(
            src_ref=src,
            dst_ref=dst,
            send_sem=self.sems.at[0, self.used],
            recv_sem=self.sems.at[1, self.used],
            device_id=other,
            device_id_type=MESH,
        )
        self.used += 1
        copy.start()
        return copy


def take_turns(tasks):
    tasks = list(tasks)
    while tasks:
        for task in list(tasks):
            try:
                next(task)
            except StopIteration:
                tasks.remove(task)


def halvings(first, size, distances):
    steps = []
    offset = first
    for distance in distances:
        half = size // 2
        if half % 16 == 0:
            bit = (lax.axis_index("dp") // distance) % 2
            steps.append((distance, offset + bit * half, offset + (1 - bit) * half, half, True))
            offset = offset + bit * half
            size = half
        else:
            steps.append((distance, offset, offset, size, False))
    return steps


def span(offset, rows):
    return pl.ds(pl.multiple_of(offset, 16), rows)


def sum_down(send, source, work, landing, first, steps):
    at = first
    for distance, kept, given, rows, _ in steps:
        slot = pl.ds(at, rows)
        copy = send(source.at[span(given, rows)], landing.at[slot], {"dp": mirror(distance)})
        yield
        copy.wait()
        mine = source[span(kept, rows)].astype(F32)
        work[span(kept, rows)] = (mine + landing[slot].astype(F32)).astype(BF16)
        source = work
        at += rows


def spread_up(send, work, steps):
    for distance, kept, _, rows, halved in reversed(steps):
        if halved:
            region = work.at[span(kept, rows)]
            copy = send(region, region, {"dp": mirror(distance)})
            yield
            copy.wait()


def sum_all(send, source, work, result, landing, first, steps):
    yield from sum_down(send, source, work, landing, first, steps)
    _, kept, _, rows, _ = steps[-1]
    result[span(kept, rows)] = work[span(kept, rows)]
    yield from spread_up(send, result, steps)


def reduce_share(send, part, near_in, out_buf, far_in, prepare=None):
    here, near, far, diag = places()
    ready = prepare or (lambda image, start: None)
    ready(diag, True)
    first = send(part.at[diag], near_in.at[0], {"tensor": near})
    ready(near, False)
    second = send(part.at[near], near_in.at[1], {"tensor": near})
    yield
    ready(far, False)
    first.wait_recv()
    out_buf[...] = (part[far].astype(F32) + near_in[0].astype(F32)).astype(BF16)
    third = send(out_buf, far_in, {"tensor": far})
    ready(here, False)
    yield
    second.wait_recv()
    near_sum = part[here].astype(F32) + near_in[1].astype(F32)
    third.wait_recv()
    total = near_sum + far_in[...].astype(F32)
    first.wait_send()
    second.wait_send()
    third.wait_send()
    return total


def gather_share(send, out):
    here, near, far, diag = places()
    first = send(out.at[here], out.at[here], {"tensor": far})
    second = send(out.at[here], out.at[here], {"tensor": near})
    yield
    first.wait_recv()
    third = send(out.at[far], out.at[far], {"tensor": near})
    yield
    second.wait_recv()
    third.wait_recv()
    first.wait_send()
    second.wait_send()
    third.wait_send()


def tensor_others():
    _, near, far, _ = places()
    return [{"tensor": near}, {"tensor": far}]


def dp_distances(count):
    return [1 << i for i in range(count.bit_length() - 1)]


def streams(rows, count, parts):
    one = dp_distances(count)
    orders = [one, one[1:] + one[:1]]
    size = rows // parts
    found, at = [], 0
    for index in range(parts):
        steps = halvings(index * size, size, orders[index % 2])
        found.append((at, steps))
        at += sum(step[3] for step in steps)
    return found, at


def middle_kernel(part, x_ref, bias, gain, shift, out, h_ref, near_in, out_buf, far_in, sems):
    here, near, far, _ = places()
    send = Sender(sems)
    greet(tensor_others())

    def task():
        total = yield from reduce_share(send, part, near_in, out_buf, far_in)
        resid = x_ref[here].astype(F32) + total + line(bias)
        h_ref[...] = resid
        hat, _ = normalize(resid)
        out[here] = (hat * line(gain) + line(shift)).astype(BF16)
        yield from gather_share(send, out)

    take_turns([task()])


def turn_kernel(
    count, part, h_ref, g_ref, gain, fc, out, dh_ref, small, work,
    near_in, out_buf, far_in, sems, landing,
):
    here = lax.axis_index("tensor")
    send = Sender(sems)
    greet(tensor_others() + [{"dp": mirror(d)} for d in dp_distances(count)])
    found, _ = streams(fc.shape[0], count, 4)

    def task():
        grad = yield from reduce_share(send, part, near_in, out_buf, far_in)
        own = g_ref[here].astype(F32)
        hat, scale = normalize(h_ref[...])
        grad_resid = own + norm_back(hat, scale, line(gain), grad)
        dh_ref[...] = grad_resid
        out[here] = grad_resid.astype(BF16)
        small[0:1] = jnp.sum(grad * hat, axis=0, keepdims=True)
        small[1:2] = jnp.sum(grad, axis=0, keepdims=True)
        small[2:3] = jnp.sum(grad_resid, axis=0, keepdims=True)
        small[3:4] = jnp.sum(own, axis=0, keepdims=True)
        small[4:8] = jnp.zeros((4, small.shape[1]), F32)
        yield from gather_share(send, out)

    take_turns([
        task(),
        *(sum_down(send, fc, work, landing, at, steps) for at, steps in found),
    ])


def last_kernel(
    count, length, grads_in, mixed, normed, query, keys, values, wp, wq, wk, wv,
    x_ref, dh_ref, gain, small_in, bfc1, fc, branch, h_ref, bias_out,
    out, small, fc_out, heads_out, layer,
    near_in, out_buf, far_in, sems, near_two, out_two, far_two, part, acc, bias, heads, work, landing, sums, got,
):
    here, near, far, _ = places()
    send = Sender(sems)
    distances = dp_distances(count)
    greet(tensor_others() + [{"dp": mirror(d)} for d in distances])
    local = wp.shape[0]
    fc_streams, _ = streams(fc.shape[0], count, 4)
    head_streams, _ = streams(heads.shape[0], count, 2)
    for _, steps in fc_streams:
        _, kept, _, rows, _ = steps[-1]
        fc_out[span(kept, rows)] = fc[span(kept, rows)]
    sums[0, 8:16] = jnp.zeros((8, sums.shape[2]), F32)

    def prepare(image, start):
        image_back(
            length, image, start, grads_in, mixed, normed, query, keys, values,
            wp, wq, wk, wv, part, bias, acc,
        )

    def task():
        total = yield from reduce_share(send, part, near_in, out_buf, far_in, prepare)
        hat, scale = normalize(x_ref[here].astype(F32))
        out[here] = (dh_ref[...] + norm_back(hat, scale, line(gain), total)).astype(BF16)
        sums[0, :8] = small_in[...]
        sums[0, 4:5] = jnp.sum(total * hat, axis=0, keepdims=True)
        sums[0, 5:6] = jnp.sum(total, axis=0, keepdims=True)
        copy = send(sums.at[0], got.at[0], {"tensor": near})
        yield from gather_share(send, out)
        copy.wait()
        sums[1] = sums[0] + got[0]
        copy = send(sums.at[1], got.at[1], {"tensor": far})
        yield
        copy.wait()
        sums[2] = sums[1] + got[1]
        sums[2, 8:9] = bfc1[...]
        sums[2, 9:11, :local] = bias[...]
        for slot, distance in enumerate(distances, 2):
            copy = send(sums.at[slot], got.at[slot], {"dp": mirror(distance)})
            yield
            copy.wait()
            sums[slot + 1] = sums[slot] + got[slot]
        small[...] = sums[len(distances) + 2]

    def layer_task():
        total = yield from reduce_share(send, branch, near_two, out_two, far_two)
        layer[here] = (h_ref[...] + total + line(bias_out)).astype(BF16)
        yield from gather_share(send, layer)

    def head_task(index, at, steps):
        yield
        if index == 0:
            for block in range(4):
                heads[block * local : (block + 1) * local] = acc[block].astype(BF16)
        yield from sum_all(send, heads, work, heads_out, landing, at, steps)

    take_turns([
        *(spread_up(send, fc_out, steps) for _, steps in fc_streams),
        layer_task(),
        task(),
        *(head_task(i, at, steps) for i, (at, steps) in enumerate(head_streams)),
    ])


def whole(count):
    return [pl.BlockSpec(memory_space=pltpu.VMEM)] * count


def fixed(shape):
    return pl.BlockSpec(shape, lambda step: (0,) * len(shape))


def each(shape):
    return pl.BlockSpec((1,) + shape[1:], lambda step: (step,) + (0,) * (len(shape) - 1))


def struct(shape, dtype):
    return jax.ShapeDtypeStruct(shape, dtype)


def exchange(kernel, number, name, outs, rows, width, extra, args):
    return pl.pallas_call(
        kernel,
        out_shape=outs,
        in_specs=whole(len(args)),
        out_specs=whole(len(outs)),
        scratch_shapes=[
            pltpu.VMEM((2, rows, width), BF16),
            pltpu.VMEM((rows, width), BF16),
            pltpu.VMEM((rows, width), BF16),
            pltpu.SemaphoreType.DMA((2, 64)),
            *extra,
        ],
        compiler_params=pltpu.CompilerParams(
            collective_id=number, has_side_effects=True, vmem_limit_bytes=VMEM_LIMIT
        ),
        cost_estimate=pl.CostEstimate(
            flops=0, bytes_accessed=50_000_000, transcendentals=0
        ),
        name=name,
    )(*args)


def stepped(kernel, name, steps, args, arg_specs, outs, out_specs, scratch, flops):
    return pl.pallas_call(
        kernel,
        grid=(steps,),
        out_shape=outs,
        in_specs=arg_specs,
        out_specs=out_specs,
        scratch_shapes=scratch,
        compiler_params=pltpu.CompilerParams(vmem_limit_bytes=VMEM_LIMIT),
        cost_estimate=pl.CostEstimate(
            flops=flops, bytes_accessed=20_000_000, transcendentals=0
        ),
        name=name,
    )(*args)


def shards(
    tokens, ln1_gain, ln1_shift, w_query, b_query, w_key, w_value, b_value, w_proj, b_proj,
    ln2_gain, ln2_shift, w_fc1, b_fc1, w_fc2, b_fc2, cotangent,
):
    images, length, width = tokens.shape
    assert images == lax.axis_size("tensor") == 4
    local = w_query.shape[1]
    hidden = w_fc1.shape[1]
    rows = (length + 15) // 16 * 16
    pad = ((0, 0), (0, rows - length), (0, 0))
    x = jnp.pad(tokens, pad)
    g = jnp.pad(cotangent, pad)
    full = (images, rows, width)
    thin = (images, rows, local)
    count = lax.axis_size("dp")
    distances = dp_distances(count)
    assert hidden == width and 4 * local == width and 1 << len(distances) == count
    turned = [weight.T for weight in (w_query, w_key, w_value)]

    normed, query, keys, values, mixed, part = stepped(
        lambda *refs: attention_kernel(length, *refs), "attention", images,
        (x, ln1_gain, ln1_shift, b_query, b_value, *turned, w_proj),
        [each(full)] + [fixed((width,))] * 2 + [fixed((local,))] * 2
        + [fixed((local, width))] * 4,
        [struct(full, BF16)] + [struct(thin, BF16)] * 4 + [struct(full, BF16)],
        [each(full)] + [each(thin)] * 4 + [each(full)],
        [], 2_000_000_000,
    )
    middle, resid = exchange(
        middle_kernel, 0, "middle", [struct(full, BF16), struct((rows, width), F32)], rows, width,
        [], (part, x, b_proj, ln2_gain, ln2_shift),
    )
    part, branch, fc, grad_bfc1 = stepped(
        feed_kernel, "feed", images,
        (middle, g, w_fc1, b_fc1, w_fc2),
        [each(full), each(full), fixed((width, hidden)), fixed((hidden,)),
         fixed((hidden, width))],
        [struct(full, BF16)] * 2
        + [struct((width + hidden, width), BF16), struct((1, hidden), F32)],
        [each(full), each(full), fixed((width + hidden, width)), fixed((1, hidden))],
        [pltpu.VMEM((width, hidden), F32), pltpu.VMEM((hidden, width), F32)], 6_000_000_000,
    )
    _, land = streams(width + hidden, count, 4)
    grads_in, grad_resid, small, fc = exchange(
        lambda *refs: turn_kernel(count, *refs), 1, "turn",
        [struct(full, BF16), struct((rows, width), F32), struct((8, width), F32),
         struct(fc.shape, BF16)],
        rows, width, [pltpu.VMEM((land, width), BF16)],
        (part, resid, g, ln2_gain, fc),
    )
    _, land = streams(width, count, 2)
    out, small, fc, heads, layer_out = exchange(
        lambda *refs: last_kernel(count, length, *refs), 2, "last",
        [struct(full, BF16), struct((16, width), F32), struct(fc.shape, BF16),
         struct((width, width), BF16), struct(full, BF16)],
        rows, width,
        [pltpu.VMEM((2, rows, width), BF16), pltpu.VMEM((rows, width), BF16),
         pltpu.VMEM((rows, width), BF16), pltpu.VMEM(full, BF16), pltpu.VMEM((4, local, width), F32),
         pltpu.VMEM((2, local), F32), pltpu.VMEM((width, width), BF16),
         pltpu.VMEM((width, width), BF16), pltpu.VMEM((land, width), BF16),
         pltpu.VMEM((3 + len(distances), 16, width), F32),
         pltpu.VMEM((2 + len(distances), 16, width), F32)],
        (grads_in, mixed, normed, query, keys, values, w_proj, *turned,
         x, grad_resid, ln1_gain, small, grad_bfc1, fc, branch, resid, b_fc2),
    )
    tokens_grad = out[:, :length]
    layer_out = layer_out[:, :length]
    heads = heads.astype(F32)
    fc = fc.astype(F32)
    square = lambda i: heads[i * local : (i + 1) * local]
    return (
        layer_out,
        tokens_grad,
        small[4],
        small[5],
        square(0).T,
        small[9, :local],
        square(1).T,
        square(2).T,
        small[10, :local],
        square(3),
        small[2],
        small[0],
        small[1],
        fc[:width],
        small[8, :hidden],
        fc[width:],
        small[3],
    )


def solution(mesh):
    in_specs = (
        P("dp", None, None),
        P(),
        P(),
        P(None, "tensor"),
        P("tensor"),
        P(None, "tensor"),
        P(None, "tensor"),
        P("tensor"),
        P("tensor", None),
        P(),
        P(),
        P(),
        P(None, "tensor"),
        P("tensor"),
        P("tensor", None),
        P(),
        P("dp", None, None),
    )
    out_specs = (
        P("dp", None, None),
        P("dp", None, None),
        P(),
        P(),
        P(None, "tensor"),
        P("tensor"),
        P(None, "tensor"),
        P(None, "tensor"),
        P("tensor"),
        P("tensor", None),
        P(),
        P(),
        P(),
        P(None, "tensor"),
        P("tensor"),
        P("tensor", None),
        P(),
    )
    return jax.shard_map(shards, mesh=mesh, in_specs=in_specs, out_specs=out_specs, check_vma=False)
```

```python
import jax
import jax.numpy as jnp
from jax import lax
from jax.experimental import pallas as pl
from jax.experimental.pallas import tpu as pltpu
from jax.sharding import PartitionSpec as P

HEAD_DIM = 64
EPSILON = 1e-06
BF16 = jnp.bfloat16
F32 = jnp.float32
MESH = pl.DeviceIdType.MESH
VMEM_LIMIT = 56 * 1024 * 1024


def matmul(left, right):
    return jnp.dot(left, right, preferred_element_type=F32)


def inner_rows(left, right):
    return lax.dot_general(left, right, (((0,), (0,)), ((), ())), preferred_element_type=F32)


def times_transpose(left, right):
    return lax.dot_general(left, right, (((1,), (1,)), ((), ())), preferred_element_type=F32)


def normalize(values):
    center = values - jnp.mean(values, axis=-1, keepdims=True)
    scale = lax.rsqrt(jnp.mean(center * center, axis=-1, keepdims=True) + EPSILON)
    return center * scale, scale


def norm_back(hat, scale, gain, grad):
    inner = grad * gain
    return scale * (
        inner
        - jnp.mean(inner, axis=-1, keepdims=True)
        - hat * jnp.mean(inner * hat, axis=-1, keepdims=True)
    )


def line(ref):
    return ref[...].reshape(1, ref.shape[0])


def soft_probs(query, keys, length):
    scores = times_transpose(query, keys) * (HEAD_DIM**-0.5)
    column = lax.broadcasted_iota(jnp.int32, scores.shape, 1)
    scores = jnp.where(column < length, scores, -1e30)
    raised = jnp.exp(scores - jnp.max(scores, axis=-1, keepdims=True))
    return raised * (1.0 / jnp.sum(raised, axis=-1, keepdims=True))


def attention_kernel(
    length, x_ref, gain, shift, bq, bv, wq, wk, wv, wp, a_ref, q_ref, k_ref, v_ref, o_ref, part_ref
):
    hat, _ = normalize(x_ref[0].astype(F32))
    normed = (hat * line(gain) + line(shift)).astype(BF16)
    a_ref[0] = normed
    query = (times_transpose(normed, wq[...]) + line(bq)).astype(BF16)
    keys = times_transpose(normed, wk[...]).astype(BF16)
    values = (times_transpose(normed, wv[...]) + line(bv)).astype(BF16)
    q_ref[0] = query
    k_ref[0] = keys
    v_ref[0] = values
    heads = []
    for head in range(query.shape[1] // HEAD_DIM):
        cols = slice(head * HEAD_DIM, (head + 1) * HEAD_DIM)
        probs = soft_probs(query[:, cols], keys[:, cols], length)
        heads.append(matmul(probs.astype(BF16), values[:, cols]))
    mixed = jnp.concatenate(heads, axis=1).astype(BF16)
    o_ref[0] = mixed
    part_ref[0] = matmul(mixed, wp[...]).astype(BF16)


def feed_kernel(c_ref, g_ref, w1, b1, w2, part_ref, branch_ref, fc_ref, bias_ref, acc1, acc2):
    step = pl.program_id(0)
    width = c_ref.shape[2]

    @pl.when(step == 0)
    def _():
        acc1[...] = jnp.zeros_like(acc1)
        acc2[...] = jnp.zeros_like(acc2)
        bias_ref[...] = jnp.zeros_like(bias_ref)

    middle = c_ref[0]
    grad = g_ref[0]
    hidden = matmul(middle, w1[...]) + line(b1)
    cdf = 0.5 * (1.0 + lax.erf(hidden * (0.5**0.5)))
    slope = cdf + hidden * jnp.exp(-0.5 * hidden * hidden) * 0.3989422804014327
    active = (hidden * cdf).astype(BF16)
    grad_hidden = (times_transpose(grad, w2[...]) * slope).astype(BF16)
    branch_ref[0] = matmul(active, w2[...]).astype(BF16)
    part_ref[0] = times_transpose(grad_hidden, w1[...]).astype(BF16)
    acc2[...] += inner_rows(active, grad)
    acc1[...] += inner_rows(middle, grad_hidden)
    bias_ref[...] += jnp.sum(grad_hidden.astype(F32), axis=0, keepdims=True)

    @pl.when(step == pl.num_programs(0) - 1)
    def _():
        fc_ref[:width] = acc1[...].astype(BF16)
        fc_ref[width:] = acc2[...].astype(BF16)


def image_back(
    length, image, start, h_ref, o_ref, a_ref, q_ref, k_ref, v_ref, wp, wq, wk, wv,
    part_ref, bias_ref, acc,
):
    def add(ref, index, value):
        ref[index] = value if start else ref[index] + value

    low = h_ref[image]
    add(acc, 3, inner_rows(o_ref[image], low))
    grad_mixed = times_transpose(low, wp[...]).astype(BF16)
    normed = a_ref[image]
    query, keys, values = q_ref[image], k_ref[image], v_ref[image]
    score_scale = HEAD_DIM**-0.5
    dq, dk, dv = [], [], []
    for head in range(query.shape[1] // HEAD_DIM):
        cols = slice(head * HEAD_DIM, (head + 1) * HEAD_DIM)
        qh, kh, vh, gh = query[:, cols], keys[:, cols], values[:, cols], grad_mixed[:, cols]
        probs = soft_probs(qh, kh, length)
        dv.append(inner_rows(probs.astype(BF16), gh))
        grad_probs = times_transpose(gh, vh)
        total = jnp.sum(probs * grad_probs, axis=-1, keepdims=True)
        grad_scores = (probs * (grad_probs - total)).astype(BF16)
        dq.append(matmul(grad_scores, kh) * score_scale)
        dk.append(inner_rows(grad_scores, qh) * score_scale)
    dq = jnp.concatenate(dq, axis=1).astype(BF16)
    dk = jnp.concatenate(dk, axis=1).astype(BF16)
    dv = jnp.concatenate(dv, axis=1).astype(BF16)
    add(bias_ref, slice(0, 1), jnp.sum(dq.astype(F32), axis=0, keepdims=True))
    add(bias_ref, slice(1, 2), jnp.sum(dv.astype(F32), axis=0, keepdims=True))
    part_ref[image] = (
        matmul(dq, wq[...]) + matmul(dk, wk[...]) + matmul(dv, wv[...])
    ).astype(BF16)
    add(acc, 0, inner_rows(dq, normed))
    add(acc, 1, inner_rows(dk, normed))
    add(acc, 2, inner_rows(dv, normed))


def places():
    here = lax.axis_index("tensor")
    return here, here + 1 - 2 * (here % 2), (here + 2) % 4, 3 - here


def mirror(distance):
    me = lax.axis_index("dp")
    return me + distance - 2 * distance * ((me // distance) % 2)


def greet(others):
    barrier = pltpu.get_barrier_semaphore()
    for other in others:
        pl.semaphore_signal(barrier, inc=1, device_id=other, device_id_type=MESH)
    pl.semaphore_wait(barrier, len(others))


class Sender:
    def __init__(self, sems):
        self.sems = sems
        self.used = 0

    def __call__(self, src, dst, other):
        copy = pltpu.make_async_remote_copy(
            src_ref=src,
            dst_ref=dst,
            send_sem=self.sems.at[0, self.used],
            recv_sem=self.sems.at[1, self.used],
            device_id=other,
            device_id_type=MESH,
        )
        self.used += 1
        copy.start()
        return copy


def take_turns(tasks):
    tasks = list(tasks)
    while tasks:
        for task in list(tasks):
            try:
                next(task)
            except StopIteration:
                tasks.remove(task)


def halvings(first, size, distances):
    steps = []
    offset = first
    for distance in distances:
        half = size // 2
        if half % 16 == 0:
            bit = (lax.axis_index("dp") // distance) % 2
            steps.append((distance, offset + bit * half, offset + (1 - bit) * half, half, True))
            offset = offset + bit * half
            size = half
        else:
            steps.append((distance, offset, offset, size, False))
    return steps


def span(offset, rows):
    return pl.ds(pl.multiple_of(offset, 16), rows)


def sum_down(send, source, work, landing, first, steps):
    at = first
    for distance, kept, given, rows, _ in steps:
        slot = pl.ds(at, rows)
        copy = send(source.at[span(given, rows)], landing.at[slot], {"dp": mirror(distance)})
        yield
        copy.wait()
        mine = source[span(kept, rows)].astype(F32)
        work[span(kept, rows)] = (mine + landing[slot].astype(F32)).astype(BF16)
        source = work
        at += rows


def spread_up(send, work, steps):
    for distance, kept, _, rows, halved in reversed(steps):
        if halved:
            region = work.at[span(kept, rows)]
            copy = send(region, region, {"dp": mirror(distance)})
            yield
            copy.wait()


def sum_all(send, source, work, result, landing, first, steps):
    yield from sum_down(send, source, work, landing, first, steps)
    _, kept, _, rows, _ = steps[-1]
    result[span(kept, rows)] = work[span(kept, rows)]
    yield from spread_up(send, result, steps)


def reduce_share(send, part, near_in, out_buf, far_in, prepare=None):
    here, near, far, diag = places()
    ready = prepare or (lambda image, start: None)
    ready(diag, True)
    first = send(part.at[diag], near_in.at[0], {"tensor": near})
    ready(near, False)
    second = send(part.at[near], near_in.at[1], {"tensor": near})
    yield
    ready(far, False)
    first.wait_recv()
    out_buf[...] = (part[far].astype(F32) + near_in[0].astype(F32)).astype(BF16)
    third = send(out_buf, far_in, {"tensor": far})
    ready(here, False)
    yield
    second.wait_recv()
    near_sum = part[here].astype(F32) + near_in[1].astype(F32)
    third.wait_recv()
    total = near_sum + far_in[...].astype(F32)
    first.wait_send()
    second.wait_send()
    third.wait_send()
    return total


def gather_share(send, out):
    here, near, far, diag = places()
    first = send(out.at[here], out.at[here], {"tensor": far})
    second = send(out.at[here], out.at[here], {"tensor": near})
    yield
    first.wait_recv()
    third = send(out.at[far], out.at[far], {"tensor": near})
    yield
    second.wait_recv()
    third.wait_recv()
    first.wait_send()
    second.wait_send()
    third.wait_send()


def tensor_others():
    _, near, far, _ = places()
    return [{"tensor": near}, {"tensor": far}]


def dp_distances(count):
    return [1 << i for i in range(count.bit_length() - 1)]


def streams(rows, count, parts):
    one = dp_distances(count)
    orders = [one, one[1:2] + one[:1] + one[2:]]
    size = rows // parts
    found, at = [], 0
    for index in range(parts):
        steps = halvings(index * size, size, orders[index % 2])
        found.append((at, steps))
        at += sum(step[3] for step in steps)
    return found, at


def middle_kernel(part, x_ref, bias, gain, shift, out, h_ref, near_in, out_buf, far_in, sems):
    here, near, far, _ = places()
    send = Sender(sems)
    greet(tensor_others())

    def task():
        total = yield from reduce_share(send, part, near_in, out_buf, far_in)
        resid = x_ref[here].astype(F32) + total + line(bias)
        h_ref[...] = resid
        hat, _ = normalize(resid)
        out[here] = (hat * line(gain) + line(shift)).astype(BF16)
        yield from gather_share(send, out)

    take_turns([task()])


def turn_kernel(
    count, part, h_ref, g_ref, gain, fc, out, dh_ref, small, work,
    near_in, out_buf, far_in, sems, landing,
):
    here = lax.axis_index("tensor")
    send = Sender(sems)
    greet(tensor_others() + [{"dp": mirror(d)} for d in dp_distances(count)])
    found, _ = streams(fc.shape[0], count, 4)

    def task():
        grad = yield from reduce_share(send, part, near_in, out_buf, far_in)
        own = g_ref[here].astype(F32)
        hat, scale = normalize(h_ref[...])
        grad_resid = own + norm_back(hat, scale, line(gain), grad)
        dh_ref[...] = grad_resid
        out[here] = grad_resid.astype(BF16)
        small[0:1] = jnp.sum(grad * hat, axis=0, keepdims=True)
        small[1:2] = jnp.sum(grad, axis=0, keepdims=True)
        small[2:3] = jnp.sum(grad_resid, axis=0, keepdims=True)
        small[3:4] = jnp.sum(own, axis=0, keepdims=True)
        small[4:8] = jnp.zeros((4, small.shape[1]), F32)
        yield from gather_share(send, out)

    take_turns([
        task(),
        *(sum_down(send, fc, work, landing, at, steps) for at, steps in found),
    ])


def last_kernel(
    count, length, grads_in, mixed, normed, query, keys, values, wp, wq, wk, wv,
    x_ref, dh_ref, gain, small_in, bfc1, fc, branch, h_ref, bias_out,
    out, small, fc_out, heads_out, layer,
    near_in, out_buf, far_in, sems, near_two, out_two, far_two, part, acc, bias, heads, work, landing, sums, got,
):
    here, near, far, _ = places()
    send = Sender(sems)
    distances = dp_distances(count)
    greet(tensor_others() + [{"dp": mirror(d)} for d in distances])
    local = wp.shape[0]
    fc_streams, _ = streams(fc.shape[0], count, 4)
    head_streams, _ = streams(heads.shape[0], count, 2)
    for _, steps in fc_streams:
        _, kept, _, rows, _ = steps[-1]
        fc_out[span(kept, rows)] = fc[span(kept, rows)]
    sums[0, 8:16] = jnp.zeros((8, sums.shape[2]), F32)

    def prepare(image, start):
        image_back(
            length, image, start, grads_in, mixed, normed, query, keys, values,
            wp, wq, wk, wv, part, bias, acc,
        )

    def task():
        total = yield from reduce_share(send, part, near_in, out_buf, far_in, prepare)
        hat, scale = normalize(x_ref[here].astype(F32))
        out[here] = (dh_ref[...] + norm_back(hat, scale, line(gain), total)).astype(BF16)
        sums[0, :8] = small_in[...]
        sums[0, 4:5] = jnp.sum(total * hat, axis=0, keepdims=True)
        sums[0, 5:6] = jnp.sum(total, axis=0, keepdims=True)
        copy = send(sums.at[0], got.at[0], {"tensor": near})
        yield from gather_share(send, out)
        copy.wait()
        sums[1] = sums[0] + got[0]
        copy = send(sums.at[1], got.at[1], {"tensor": far})
        yield
        copy.wait()
        sums[2] = sums[1] + got[1]
        sums[2, 8:9] = bfc1[...]
        sums[2, 9:11, :local] = bias[...]
        for slot, distance in enumerate(distances, 2):
            copy = send(sums.at[slot], got.at[slot], {"dp": mirror(distance)})
            yield
            copy.wait()
            sums[slot + 1] = sums[slot] + got[slot]
        small[...] = sums[len(distances) + 2]

    def layer_task():
        total = yield from reduce_share(send, branch, near_two, out_two, far_two)
        layer[here] = (h_ref[...] + total + line(bias_out)).astype(BF16)
        yield from gather_share(send, layer)

    def head_task(index, at, steps):
        yield
        if index == 0:
            for block in range(4):
                heads[block * local : (block + 1) * local] = acc[block].astype(BF16)
        yield from sum_all(send, heads, work, heads_out, landing, at, steps)

    take_turns([
        *(spread_up(send, fc_out, steps) for _, steps in fc_streams),
        layer_task(),
        task(),
        *(head_task(i, at, steps) for i, (at, steps) in enumerate(head_streams)),
    ])


def whole(count):
    return [pl.BlockSpec(memory_space=pltpu.VMEM)] * count


def fixed(shape):
    return pl.BlockSpec(shape, lambda step: (0,) * len(shape))


def each(shape):
    return pl.BlockSpec((1,) + shape[1:], lambda step: (step,) + (0,) * (len(shape) - 1))


def struct(shape, dtype):
    return jax.ShapeDtypeStruct(shape, dtype)


def exchange(kernel, number, name, outs, rows, width, extra, args):
    return pl.pallas_call(
        kernel,
        out_shape=outs,
        in_specs=whole(len(args)),
        out_specs=whole(len(outs)),
        scratch_shapes=[
            pltpu.VMEM((2, rows, width), BF16),
            pltpu.VMEM((rows, width), BF16),
            pltpu.VMEM((rows, width), BF16),
            pltpu.SemaphoreType.DMA((2, 64)),
            *extra,
        ],
        compiler_params=pltpu.CompilerParams(
            collective_id=number, has_side_effects=True, vmem_limit_bytes=VMEM_LIMIT
        ),
        cost_estimate=pl.CostEstimate(
            flops=0, bytes_accessed=50_000_000, transcendentals=0
        ),
        name=name,
    )(*args)


def stepped(kernel, name, steps, args, arg_specs, outs, out_specs, scratch, flops):
    return pl.pallas_call(
        kernel,
        grid=(steps,),
        out_shape=outs,
        in_specs=arg_specs,
        out_specs=out_specs,
        scratch_shapes=scratch,
        compiler_params=pltpu.CompilerParams(vmem_limit_bytes=VMEM_LIMIT),
        cost_estimate=pl.CostEstimate(
            flops=flops, bytes_accessed=20_000_000, transcendentals=0
        ),
        name=name,
    )(*args)


def shards(
    tokens, ln1_gain, ln1_shift, w_query, b_query, w_key, w_value, b_value, w_proj, b_proj,
    ln2_gain, ln2_shift, w_fc1, b_fc1, w_fc2, b_fc2, cotangent,
):
    images, length, width = tokens.shape
    assert images == lax.axis_size("tensor") == 4
    local = w_query.shape[1]
    hidden = w_fc1.shape[1]
    rows = (length + 15) // 16 * 16
    pad = ((0, 0), (0, rows - length), (0, 0))
    x = jnp.pad(tokens, pad)
    g = jnp.pad(cotangent, pad)
    full = (images, rows, width)
    thin = (images, rows, local)
    count = lax.axis_size("dp")
    distances = dp_distances(count)
    assert hidden == width and 4 * local == width and 1 << len(distances) == count
    turned = [weight.T for weight in (w_query, w_key, w_value)]

    normed, query, keys, values, mixed, part = stepped(
        lambda *refs: attention_kernel(length, *refs), "attention", images,
        (x, ln1_gain, ln1_shift, b_query, b_value, *turned, w_proj),
        [each(full)] + [fixed((width,))] * 2 + [fixed((local,))] * 2
        + [fixed((local, width))] * 4,
        [struct(full, BF16)] + [struct(thin, BF16)] * 4 + [struct(full, BF16)],
        [each(full)] + [each(thin)] * 4 + [each(full)],
        [], 2_000_000_000,
    )
    middle, resid = exchange(
        middle_kernel, 0, "middle", [struct(full, BF16), struct((rows, width), F32)], rows, width,
        [], (part, x, b_proj, ln2_gain, ln2_shift),
    )
    part, branch, fc, grad_bfc1 = stepped(
        feed_kernel, "feed", images,
        (middle, g, w_fc1, b_fc1, w_fc2),
        [each(full), each(full), fixed((width, hidden)), fixed((hidden,)),
         fixed((hidden, width))],
        [struct(full, BF16)] * 2
        + [struct((width + hidden, width), BF16), struct((1, hidden), F32)],
        [each(full), each(full), fixed((width + hidden, width)), fixed((1, hidden))],
        [pltpu.VMEM((width, hidden), F32), pltpu.VMEM((hidden, width), F32)], 6_000_000_000,
    )
    _, land = streams(width + hidden, count, 4)
    grads_in, grad_resid, small, fc = exchange(
        lambda *refs: turn_kernel(count, *refs), 1, "turn",
        [struct(full, BF16), struct((rows, width), F32), struct((8, width), F32),
         struct(fc.shape, BF16)],
        rows, width, [pltpu.VMEM((land, width), BF16)],
        (part, resid, g, ln2_gain, fc),
    )
    _, land = streams(width, count, 2)
    out, small, fc, heads, layer_out = exchange(
        lambda *refs: last_kernel(count, length, *refs), 2, "last",
        [struct(full, BF16), struct((16, width), F32), struct(fc.shape, BF16),
         struct((width, width), BF16), struct(full, BF16)],
        rows, width,
        [pltpu.VMEM((2, rows, width), BF16), pltpu.VMEM((rows, width), BF16),
         pltpu.VMEM((rows, width), BF16), pltpu.VMEM(full, BF16), pltpu.VMEM((4, local, width), F32),
         pltpu.VMEM((2, local), F32), pltpu.VMEM((width, width), BF16),
         pltpu.VMEM((width, width), BF16), pltpu.VMEM((land, width), BF16),
         pltpu.VMEM((3 + len(distances), 16, width), F32),
         pltpu.VMEM((2 + len(distances), 16, width), F32)],
        (grads_in, mixed, normed, query, keys, values, w_proj, *turned,
         x, grad_resid, ln1_gain, small, grad_bfc1, fc, branch, resid, b_fc2),
    )
    tokens_grad = out[:, :length]
    layer_out = layer_out[:, :length]
    heads = heads.astype(F32)
    fc = fc.astype(F32)
    square = lambda i: heads[i * local : (i + 1) * local]
    return (
        layer_out,
        tokens_grad,
        small[4],
        small[5],
        square(0).T,
        small[9, :local],
        square(1).T,
        square(2).T,
        small[10, :local],
        square(3),
        small[2],
        small[0],
        small[1],
        fc[:width],
        small[8, :hidden],
        fc[width:],
        small[3],
    )


def solution(mesh):
    in_specs = (
        P("dp", None, None),
        P(),
        P(),
        P(None, "tensor"),
        P("tensor"),
        P(None, "tensor"),
        P(None, "tensor"),
        P("tensor"),
        P("tensor", None),
        P(),
        P(),
        P(),
        P(None, "tensor"),
        P("tensor"),
        P("tensor", None),
        P(),
        P("dp", None, None),
    )
    out_specs = (
        P("dp", None, None),
        P("dp", None, None),
        P(),
        P(),
        P(None, "tensor"),
        P("tensor"),
        P(None, "tensor"),
        P(None, "tensor"),
        P("tensor"),
        P("tensor", None),
        P(),
        P(),
        P(),
        P(None, "tensor"),
        P("tensor"),
        P("tensor", None),
        P(),
    )
    return jax.shard_map(shards, mesh=mesh, in_specs=in_specs, out_specs=out_specs, check_vma=False)
```
